32 devices in a mesh: gx: 8 (over z, core), gy: 4 (over y, x).
Axes of the slice: x: 2, y: 2, z: 4, core: 2. Of those that a mesh axis runs over, the one named last changes fastest.
Arguments:
- pressure: float32 [2048, 1024], P('gx', 'gy'), may hold values from -6 to 6
- source: float32 [2048, 1024], P('gx', 'gy'), may hold values from -6 to 6
- conductivity: float32 [2048, 1024], P('gx', 'gy'), may hold values from 0.2 to 5
- storage: float32 [2048, 1024], P('gx', 'gy'), may hold values from 0.2 to 1
Outputs:
- pressure_next: float32 [2048, 1024], P('gx', 'gy')
The draws below stay inside these ranges and needn't reach their ends.
All inputs are finite; a program needn't handle non-finite values.
Results may differ from the reference program's by a relative error of at most 0.0001.
Values sent between devices are 32-bit elements; how exact they have to be, the bound alone decides.
A program may use at most 128 MiB of HBM per device.

```python
import math
import jax
import jax.numpy as jnp

LEVELS_SPLIT = 4
LEVELS_MERGED = 2
COARSE_SWEEPS = 8
NX = 2048
NY = 1024


def block_levels(own_key, shape, cuts, least, top_value):
    gain, own = 1.0, jax.random.fold_in(own_key, 6)
    for position, blocks in cuts:
        draws = jnp.exp(jax.random.uniform(jax.random.fold_in(own, position), (blocks,), jnp.float32, least / len(cuts), top_value / len(cuts)))
        gain = gain * jnp.repeat(draws, shape[position] // blocks).reshape([-1 if axis == position else 1 for axis in range(len(shape))])
    return gain


def centred(own_key, extent, deviation, limit, split=(), kind=jnp.bfloat16):
    values = deviation * jax.random.normal(own_key, extent, jnp.float32)
    if split:
        values = values * block_levels(own_key, extent, split, -0.22, 0.18)
    return jnp.clip(values, -limit, limit).astype(kind)


def setup_inputs(seed: int = 0) -> dict:
    keys = jax.random.split(jax.random.key(seed), 5)
    return {
        "pressure": centred(keys[0], (NX, NY), 1.0, 6.0, ((0, 8), (1, 4)), jnp.float32),
        "source": centred(keys[1], (NX, NY), 1.0, 6.0, ((0, 8), (1, 4)), jnp.float32),
        "conductivity": jnp.clip(jnp.exp(math.log(5.0) - 3.218876 * jax.random.uniform(keys[2], (NX, NY), jnp.float32) ** block_levels(keys[2], (NX, NY), ((0, 8), (1, 4)), -0.2, 0.2)), 0.2, 5.0),
        "storage": jnp.clip(0.2 + 0.8 * jax.random.uniform(keys[3], (NX, NY), jnp.float32) ** block_levels(keys[3], (NX, NY), ((0, 8), (1, 4)), -0.2, 0.2), 0.2, 1.0),
    }


OMEGA = 0.8


def coarsen(grid):
    height, breadth = grid.shape
    return grid.reshape(height // 2, 2, breadth // 2, 2).sum(axis=(1, 3))


def prolong(grid):
    return jnp.repeat(jnp.repeat(grid, 2, axis=0), 2, axis=1)


def face_terms(conduct, stored):
    padded = jnp.pad(conduct, 1)
    west_face = 0.5 * (conduct + padded[:-2, 1:-1])
    east_face = 0.5 * (conduct + padded[2:, 1:-1])
    south_face = 0.5 * (conduct + padded[1:-1, :-2])
    north_face = 0.5 * (conduct + padded[1:-1, 2:])
    diagonal = stored + west_face + east_face + south_face + north_face
    return (diagonal, west_face, east_face, south_face, north_face)


def operate(field, section):
    diagonal, west_face, east_face, south_face, north_face = section
    padded = jnp.pad(field, 1)
    return (diagonal * field - west_face * padded[:-2, 1:-1] - east_face * padded[2:, 1:-1]
            - south_face * padded[1:-1, :-2] - north_face * padded[1:-1, 2:])


def jacobi_sweep(field, right_side, section):
    return field + OMEGA * (right_side - operate(field, section)) / section[0]


def first_sweep(right_side, section):
    return OMEGA * right_side / section[0]


def cycle(sections, depth, right_side, start_field):
    section = sections[depth]
    if depth == len(sections) - 1:
        field = first_sweep(right_side, section)
        for _ in range(COARSE_SWEEPS - 1):
            field = jacobi_sweep(field, right_side, section)
        return field
    if start_field is None:
        field = first_sweep(right_side, section)
    else:
        field = jacobi_sweep(start_field, right_side, section)
    field = jacobi_sweep(field, right_side, section)
    residual = right_side - operate(field, section)
    correction = cycle(sections, depth + 1, coarsen(residual), None)
    field = field + prolong(correction)
    field = jacobi_sweep(field, right_side, section)
    field = jacobi_sweep(field, right_side, section)
    return field


def reference(pressure, source, conductivity, storage):
    conduct, stored = conductivity, storage
    sections = []
    for depth in range(LEVELS_SPLIT + LEVELS_MERGED):
        if depth > 0:
            conduct = 0.5 * coarsen(conduct)
            stored = coarsen(stored)
        sections.append(face_terms(conduct, stored))
    return cycle(sections, 0, source, pressure)
```

```python
import functools

import jax
import jax.numpy as jnp
from jax import lax
from jax.experimental import pallas as pl
from jax.experimental.pallas import tpu as pltpu
from jax.sharding import PartitionSpec as P

LEVELS_SPLIT = 4
LEVELS_MERGED = 2
COARSE_SWEEPS = 8
OMEGA = 0.8

LOCAL = LEVELS_SPLIT - 1
LEVELS = LEVELS_SPLIT + LEVELS_MERGED
HALO = 32
G = 8
MESH = pl.DeviceIdType.MESH
F32 = jnp.float32


def round_up(n, m):
    return -(-n // m) * m


def iota(shape, dim):
    return lax.broadcasted_iota(jnp.int32, shape, dim)


def ones_where(mask):
    return jnp.where(mask, 1.0, 0.0).astype(jnp.bfloat16)


def parts(x):
    high = x.astype(jnp.bfloat16)
    low = (x - high.astype(F32)).astype(jnp.bfloat16)
    return high, low


def dot(a, b):
    return jnp.dot(a, b, preferred_element_type=F32)


def left(matrix, x):
    high, low = parts(x)
    return dot(matrix, high) + dot(matrix, low)


def right(x, matrix):
    high, low = parts(x)
    return dot(high, matrix) + dot(low, matrix)


class Level:
    def __init__(self, depth, bx, by, nx, ny):
        self.depth = depth
        self.split = depth < LOCAL
        self.nx, self.ny = nx >> depth, ny >> depth
        if self.split:
            self.halo = HALO >> depth
            self.bx, self.by = bx >> depth, by >> depth
            self.rows = self.bx + 2 * self.halo
            self.lanes = round_up(self.by + 2 * self.halo, 128)
        else:
            self.halo = 0
            self.bx, self.by = self.nx, self.ny
            self.rows = self.nx
            self.lanes = round_up(self.ny, 128)
        for step in (32, 16, 8):
            if self.rows % step == 0:
                self.step = step
                break
        if self.lanes == 128:
            for step in (128, 80, 64):
                if self.rows % step == 0:
                    self.step = step
                    break

    def scratch(self):
        tall = pltpu.VMEM((self.rows + 2 * G, self.lanes), F32)
        flat = pltpu.VMEM((self.rows, self.lanes), F32)
        return [pltpu.VMEM((7, self.rows, self.lanes), F32), tall, tall, tall, flat, flat]

    def inside(self, start, count, mx, my):
        shape = (count, self.lanes)
        row = iota(shape, 0) + start - self.halo
        lane = iota(shape, 1)
        if not self.split:
            return lane < self.ny
        col = jnp.where(lane >= self.lanes - self.halo, lane - self.lanes, lane)
        row = row + mx * self.bx
        gap = (lane >= self.by + self.halo) & (lane < self.lanes - self.halo)
        col = col + my * self.by
        return (row >= 0) & (row < self.nx) & (col >= 0) & (col < self.ny) & ~gap


def neighbours(win, count, lanes):
    mid = win[G : G + count]
    size = count + 2 * G
    up = pltpu.roll(win, 1, 0)[G : G + count]
    down = pltpu.roll(win, size - 1, 0)[G : G + count]
    before = pltpu.roll(mid, 1, 1)
    after = pltpu.roll(mid, lanes - 1, 1)
    return mid, up, down, before, after


def loop(start, count, step, body):
    total = count // step
    if total == 1:
        body(start)
    else:
        pl.loop(0, total)(lambda i: body(pl.multiple_of(start + i * step, 8)))


def setup(level, mx, my, k_ref, s_ref, a_ref, source=None):
    count = level.step

    def body(r):
        mid, up, down, before, after = neighbours(
            k_ref[pl.ds(r, count + 2 * G), :], count, level.lanes
        )
        inside = level.inside(r, count, mx, my)
        if not level.split:
            lane = iota(mid.shape, 1)
            before = jnp.where(lane == 0, 0.0, before)
            after = jnp.where(lane == level.lanes - 1, 0.0, after)
        west, east = 0.5 * (mid + up), 0.5 * (mid + down)
        south, north = 0.5 * (mid + before), 0.5 * (mid + after)
        rows = pl.ds(r, count)
        diag = s_ref[rows, :] + west + east + south + north
        c = jnp.where(inside, OMEGA / diag, 0.0)
        a_ref[0, rows, :] = c * west
        a_ref[1, rows, :] = c * east
        if level.split:
            a_ref[2, rows, :] = c * south
            a_ref[3, rows, :] = c * north
        else:
            a_ref[2, rows, :] = jnp.where(lane == 0, 0.0, c * south)
            a_ref[3, rows, :] = jnp.where(lane == level.ny - 1, 0.0, c * north)
        a_ref[5, rows, :] = c
        a_ref[6, rows, :] = diag * (1.0 / OMEGA)
        if source is not None:
            a_ref[4, rows, :] = c * source[rows_of(r, count), :]

    loop(0, level.rows, count, body)


def rows_of(r, count):
    return pl.ds(r + G, count)


def smooth(level, src, a_ref, put, start=0, total=None):
    count = level.step

    def body(r):
        mid, up, down, before, after = neighbours(
            src[pl.ds(r, count + 2 * G), :], count, level.lanes
        )
        rows = pl.ds(r, count)
        new = (1.0 - OMEGA) * mid + a_ref[4, rows, :]
        new = new + (a_ref[0, rows, :] * up + a_ref[1, rows, :] * down)
        new = new + (a_ref[2, rows, :] * before + a_ref[3, rows, :] * after)
        put(r, rows, mid, new)

    loop(start, level.rows if total is None else total, count, body)


def sweep(level, src, dst, a_ref, start=0, total=None):
    def put(r, rows, mid, new):
        dst[rows_of(r, level.step), :] = new

    smooth(level, src, a_ref, put, start, total)


def residual(level, src, dst, a_ref):
    def put(r, rows, mid, new):
        dst[rows, :] = (new - mid) * a_ref[6, rows, :]

    smooth(level, src, a_ref, put)


def lane_map(fine, coarse, lane):
    half = lane // 2
    if fine.split:
        shift = coarse.lanes - fine.lanes // 2
        half = jnp.where(lane >= fine.lanes - fine.halo, half + shift, half)
    return half


def coarsen(fine, coarse, x):
    shape = (fine.lanes, coarse.lanes)
    cols = ones_where(lane_map(fine, coarse, iota(shape, 0)) == iota(shape, 1))
    shape = (coarse.rows, fine.rows)
    rows = ones_where(iota(shape, 0) == iota(shape, 1) // 2)
    return left(rows, right(x, cols))


def prolong(fine, coarse, mx, my, x):
    shape = (coarse.lanes, fine.lanes)
    lane = iota(shape, 1)
    if fine.split and not coarse.split:
        col = jnp.where(lane >= fine.lanes - fine.halo, lane - fine.lanes, lane)
        gap = (lane >= fine.by + fine.halo) & (lane < fine.lanes - fine.halo)
        target = jnp.where(gap, -2, col + my * fine.by + 2 * coarse.lanes) // 2 - coarse.lanes
        target = jnp.where(gap, -1, target)
    else:
        target = lane_map(fine, coarse, lane)
    cols = ones_where(iota(shape, 0) == target)
    shape = (fine.rows, coarse.rows)
    row = iota(shape, 0)
    if fine.split and not coarse.split:
        row = row - fine.halo + mx * fine.bx
        row = (row + 2 * fine.rows) // 2 - fine.rows
    else:
        row = row // 2
    rows = ones_where(row == iota(shape, 1))
    return left(rows, right(x, cols))


def block_sum(x, first, count, factor, columns, place, lanes):
    shape = (count, x.shape[0])
    row = iota(shape, 1) - first
    rows = ones_where((row >= 0) & (row < count * factor) & ((row + factor) // factor - 1 == iota(shape, 0)))
    shape = (x.shape[1], lanes)
    lane = iota(shape, 0)
    cols = ones_where((lane < columns) & (lane // factor + place == iota(shape, 1)))
    return left(rows, right(x, cols))


def kernel(levels, dx, dy, *refs):
    p_hbm, s_hbm, k_hbm, st_hbm, out_ref = refs[:5]
    ext, strip_l, strip_r, halo_l, halo_r, ga, gb, gca, gcb = refs[5:14]
    held = []
    refs = refs[14:]
    for _ in levels:
        held.append(refs[:6])
        refs = refs[6:]
    load_sem, halo_send, halo_recv, y_send, y_recv, x_send, x_recv = refs

    mx, my = lax.axis_index("gx"), lax.axis_index("gy")
    top = levels[0]
    bx, by = top.bx, top.by
    own = pl.ds(G + HALO, bx)

    loads = []
    for i, ref in enumerate((p_hbm, s_hbm, k_hbm, st_hbm)):
        loads.append(pltpu.make_async_copy(ref, ext.at[i, own, pl.ds(0, by)], load_sem.at[i]))
        loads[-1].start()

    barrier = pltpu.get_barrier_semaphore()
    corners = []
    for sx in (-1, 1):
        for sy in (-1, 1):
            ok = (mx + sx >= 0) & (mx + sx < dx) & (my + sy >= 0) & (my + sy < dy)
            corners.append((sx, sy, ok))
    for d in range(1, dx):
        pl.semaphore_signal(barrier, inc=1, device_id=(lax.rem(mx + d, dx), my), device_id_type=MESH)
    for d in range(1, dy):
        pl.semaphore_signal(barrier, inc=1, device_id=(mx, lax.rem(my + d, dy)), device_id_type=MESH)
    for sx, sy, ok in corners:
        @pl.when(ok)
        def _():
            pl.semaphore_signal(barrier, inc=1, device_id=(mx + sx, my + sy), device_id_type=MESH)

    zero = jnp.zeros((G, top.lanes), F32)
    for i in (0, 2):
        ext[i, 0:G, :] = zero
        ext[i, G + top.rows :, :] = zero
    for level, (a, v, u, k, s, r) in zip(levels, held):
        for ref in (v, u, k):
            ref[0:G, :] = jnp.zeros((G, level.lanes), F32)
            ref[G + level.rows :, :] = jnp.zeros((G, level.lanes), F32)

    for copy in loads:
        copy.wait()

    lane = iota((bx, 128), 1)
    slot = lane // HALO
    for dst, first, at in ((strip_l, 0, 0), (strip_r, by - 128, 128 - HALO)):
        packed = None
        for i in range(4):
            x = ext[i, own, pl.ds(first, 128)]
            turn = (HALO * i - at) % 128
            if turn:
                x = pltpu.roll(x, turn, 1)
            packed = x if packed is None else jnp.where(slot == i, x, packed)
        dst[...] = packed

    corner_count = sum(jnp.where(ok, 1, 0) for _, _, ok in corners)
    pl.semaphore_wait(barrier, dx - 1 + dy - 1 + corner_count)

    halos = []
    n = 0
    for sx in (-1, 0, 1):
        for sy in (-1, 0, 1):
            if sx == 0 and sy == 0:
                continue
            ok = (mx + sx >= 0) & (mx + sx < dx) & (my + sy >= 0) & (my + sy < dy)
            back = (mx - sx >= 0) & (mx - sx < dx) & (my - sy >= 0) & (my - sy < dy)
            if sy == 0:
                first = G + HALO if sx < 0 else G + bx
                there = G + HALO + bx if sx < 0 else G
                src = ext.at[:, pl.ds(first, HALO), pl.ds(0, by)]
                dst = ext.at[:, pl.ds(there, HALO), pl.ds(0, by)]
            else:
                mine, theirs = (strip_l, halo_r) if sy < 0 else (strip_r, halo_l)
                if sx == 0:
                    src, dst = mine, theirs.at[pl.ds(HALO, bx)]
                elif sx < 0:
                    src, dst = mine.at[pl.ds(0, HALO)], theirs.at[pl.ds(HALO + bx, HALO)]
                else:
                    src, dst = mine.at[pl.ds(bx - HALO, HALO)], theirs.at[pl.ds(0, HALO)]
            copy = pltpu.make_async_remote_copy(
                src_ref=src, dst_ref=dst, send_sem=halo_send.at[n], recv_sem=halo_recv.at[n],
                device_id=(mx + sx, my + sy), device_id_type=MESH,
            )
            halos.append((copy, ok, back))
            n += 1
    for copy, ok, _ in halos:
        pl.when(ok)(copy.start)

    whole = levels[LOCAL]
    factor = 1 << LOCAL
    gx_rows, gy_cols = bx // factor, by // factor
    place = my * gy_cols
    sends = []

    def over_gy(buffer, base):
        copies = []
        for d in range(1, dy):
            copies.append(pltpu.make_async_remote_copy(
                src_ref=buffer.at[my], dst_ref=buffer.at[my],
                send_sem=y_send.at[base + d], recv_sem=y_recv.at[base + d],
                device_id=(mx, lax.rem(my + d, dy)), device_id_type=MESH,
            ))
            copies[-1].start()
        sends.extend(copies)
        return copies

    def over_gx(part, base):
        copies = []
        for d in range(1, dx):
            copies.append(pltpu.make_async_remote_copy(
                src_ref=part, dst_ref=part,
                send_sem=x_send.at[base + d], recv_sem=x_recv.at[base + d],
                device_id=(lax.rem(mx + d, dx), my), device_id_type=MESH,
            ))
            copies[-1].start()
        sends.extend(copies)
        return copies

    for i, scale in ((0, 0.5 ** LOCAL), (1, 1.0)):
        x = ext[2 + i, own, pl.ds(0, by)]
        gca[my, i] = scale * block_sum(x, 0, gx_rows, factor, by, place, whole.lanes)
    coef_y = over_gy(gca, 0)

    for copy, _, back in halos:
        pl.when(back)(copy.wait_recv)

    tile = pl.ds(top.lanes - 128, 128)
    lane = iota((HALO, 128), 1)

    @pl.loop(0, top.rows // HALO)
    def _(i):
        r = pl.multiple_of(i * HALO, 8)
        inside = top.inside(r, HALO, mx, my)[:, top.lanes - 128 :]
        lower, upper = halo_l[pl.ds(r, HALO), :], halo_r[pl.ds(r, HALO), :]
        for j in range(4):
            turn_l, turn_r = (128 - HALO - HALO * j) % 128, (-HALO * j) % 128
            x = pltpu.roll(lower, turn_l, 1) if turn_l else lower
            y = pltpu.roll(upper, turn_r, 1) if turn_r else upper
            x = jnp.where(lane < HALO, y, x)
            ext[j, pl.ds(r + G, HALO), tile] = jnp.where(inside, x, 0.0)

    for edge, first in ((mx == 0, G), (mx == dx - 1, G + HALO + bx)):
        @pl.when(edge)
        def _():
            for j in range(4):
                ext[j, pl.ds(first, HALO), pl.ds(0, by)] = jnp.zeros((HALO, by), F32)

    setup(top, mx, my, ext.at[2], ext.at[3, pl.ds(G, top.rows)], held[0][0], ext.at[1])

    for copy in coef_y:
        copy.wait_recv()
    gcb[:, pl.ds(pl.multiple_of(mx * gx_rows, 8), gx_rows), :] = functools.reduce(
        lambda x, y: x + y, [gca[j] for j in range(dy)]
    )
    coef_x = over_gx(gcb.at[:, pl.ds(pl.multiple_of(mx * gx_rows, 8), gx_rows)], 0)

    def inner(level, ref):
        return ref[pl.ds(G, level.rows), :]

    for depth in range(LOCAL):
        level = levels[depth]
        a, v, u, k, s, res = held[depth]
        if depth == 0:
            sweep(level, ext.at[0], v, a)
        else:
            fine = levels[depth - 1]
            fk, fs = (ext.at[2], ext.at[3, pl.ds(G, top.rows)]) if depth == 1 else held[depth - 1][3:5]
            k[pl.ds(G, level.rows), :] = 0.5 * coarsen(fine, level, inner(fine, fk))
            s[...] = coarsen(fine, level, fs[...])
            setup(level, mx, my, k, s, a)
            first = a[5] * coarsen(fine, level, held[depth - 1][5][...])
            a[4] = first
            v[pl.ds(G, level.rows), :] = first
        sweep(level, v, u, a)
        residual(level, u, res, a)

    last = levels[LOCAL - 1]
    ga[my] = block_sum(held[LOCAL - 1][5][...], last.halo, gx_rows, 2, last.by, place, whole.lanes)
    side_y = over_gy(ga, dy)

    for copy in coef_x:
        copy.wait_recv()
    for depth in range(LOCAL, LEVELS):
        level = levels[depth]
        a, v, u, k, s, res = held[depth]
        if depth == LOCAL:
            k[pl.ds(G, level.rows), :] = gcb[0]
            s[...] = gcb[1]
        else:
            fine = levels[depth - 1]
            k[pl.ds(G, level.rows), :] = 0.5 * coarsen(fine, level, inner(fine, held[depth - 1][3]))
            s[...] = coarsen(fine, level, held[depth - 1][4][...])
        setup(level, mx, my, k, s, a)

    for copy in side_y:
        copy.wait_recv()
    part = pl.ds(pl.multiple_of(mx * gx_rows, 8), gx_rows)
    gb[part, :] = functools.reduce(lambda x, y: x + y, [ga[j] for j in range(dy)])
    side_x = over_gx(gb.at[part], dx)
    for copy in side_x:
        copy.wait_recv()

    for depth in range(LOCAL, LEVELS):
        level = levels[depth]
        a, v, u, k, s, res = held[depth]
        side = gb[...] if depth == LOCAL else coarsen(levels[depth - 1], level, held[depth - 1][5][...])
        first = a[5] * side
        a[4] = first
        v[pl.ds(G, level.rows), :] = first
        if depth < LEVELS - 1:
            sweep(level, v, u, a)
            residual(level, u, res, a)
        else:
            for i in range(COARSE_SWEEPS - 1):
                sweep(level, *((v, u) if i % 2 == 0 else (u, v)), a)
            if COARSE_SWEEPS % 2:
                u[...] = v[...]

    for depth in reversed(range(LEVELS - 1)):
        level, below = levels[depth], levels[depth + 1]
        a, v, u, k, s, res = held[depth]
        u[pl.ds(G, level.rows), :] += prolong(level, below, mx, my, inner(below, held[depth + 1][2]))
        if depth:
            sweep(level, u, v, a)
            sweep(level, v, u, a)
        else:
            step = level.step
            sweep(level, u, v, a, HALO - step, bx + 2 * step)

            def put(r, rows, mid, new):
                out_ref[pl.ds(pl.multiple_of(r - HALO, 8), step), :] = new[:, :by]

            smooth(level, v, a, put, HALO, bx)

    for copy, ok, _ in halos:
        pl.when(ok)(copy.wait_send)
    for copy in sends:
        copy.wait_send()


def per_device(nx, ny, pressure, source, conductivity, storage):
    dx, dy = lax.axis_size("gx"), lax.axis_size("gy")
    bx, by = pressure.shape
    levels = [Level(depth, bx, by, nx, ny) for depth in range(LEVELS)]
    top, whole = levels[0], levels[LOCAL]
    rows = bx >> LOCAL
    scratch = [
        pltpu.VMEM((4, top.rows + 2 * G, top.lanes), F32),
        pltpu.VMEM((bx, 128), F32),
        pltpu.VMEM((bx, 128), F32),
        pltpu.VMEM((top.rows, 128), F32),
        pltpu.VMEM((top.rows, 128), F32),
        pltpu.VMEM((dy, rows, whole.lanes), F32),
        pltpu.VMEM((whole.rows, whole.lanes), F32),
        pltpu.VMEM((dy, 2, rows, whole.lanes), F32),
        pltpu.VMEM((2, whole.rows, whole.lanes), F32),
    ]
    for level in levels:
        scratch += level.scratch()
    scratch += [
        pltpu.SemaphoreType.DMA((4,)),
        pltpu.SemaphoreType.DMA((8,)),
        pltpu.SemaphoreType.DMA((8,)),
        pltpu.SemaphoreType.DMA((2 * dy,)),
        pltpu.SemaphoreType.DMA((2 * dy,)),
        pltpu.SemaphoreType.DMA((2 * dx,)),
        pltpu.SemaphoreType.DMA((2 * dx,)),
    ]
    return pl.pallas_call(
        functools.partial(kernel, levels, dx, dy),
        out_shape=jax.ShapeDtypeStruct((bx, by), F32),
        in_specs=[pl.BlockSpec(memory_space=pl.ANY)] * 4,
        out_specs=pl.BlockSpec(memory_space=pltpu.VMEM),
        scratch_shapes=scratch,
        compiler_params=pltpu.CompilerParams(
            collective_id=0, has_side_effects=True, vmem_limit_bytes=48 * 2**20
        ),
    )(pressure, source, conductivity, storage)


def solution(mesh):
    placed = (P("gx", "gy"), P("gx", "gy"), P("gx", "gy"), P("gx", "gy"))

    def run(pressure, source, conductivity, storage):
        nx, ny = pressure.shape
        return jax.shard_map(
            functools.partial(per_device, nx, ny),
            mesh=mesh, in_specs=placed, out_specs=P("gx", "gy"), check_vma=False,
        )(pressure, source, conductivity, storage)

    return run
```

```python
import functools

import jax
import jax.numpy as jnp
from jax import lax
from jax.experimental import pallas as pl
from jax.experimental.pallas import tpu as pltpu
from jax.sharding import PartitionSpec as P

LEVELS_SPLIT = 4
LEVELS_MERGED = 2
COARSE_SWEEPS = 8
OMEGA = 0.8

LOCAL = LEVELS_SPLIT - 1
LEVELS = LEVELS_SPLIT + LEVELS_MERGED
HALO = 32
G = 8
MESH = pl.DeviceIdType.MESH
F32 = jnp.float32


def round_up(n, m):
    return -(-n // m) * m


def iota(shape, dim):
    return lax.broadcasted_iota(jnp.int32, shape, dim)


def ones_where(mask):
    return jnp.where(mask, 1.0, 0.0).astype(jnp.bfloat16)


def parts(x):
    high = x.astype(jnp.bfloat16)
    low = (x - high.astype(F32)).astype(jnp.bfloat16)
    return high, low


def dot(a, b):
    return jnp.dot(a, b, preferred_element_type=F32)


def left(matrix, x):
    high, low = parts(x)
    return dot(matrix, high) + dot(matrix, low)


def right(x, matrix):
    high, low = parts(x)
    return dot(high, matrix) + dot(low, matrix)


class Level:
    def __init__(self, depth, bx, by, nx, ny):
        self.depth = depth
        self.split = depth < LOCAL
        self.nx, self.ny = nx >> depth, ny >> depth
        if self.split:
            self.halo = HALO >> depth
            self.bx, self.by = bx >> depth, by >> depth
            self.rows = self.bx + 2 * self.halo
            self.lanes = round_up(self.by + 2 * self.halo, 128)
        else:
            self.halo = 0
            self.bx, self.by = self.nx, self.ny
            self.rows = self.nx
            self.lanes = round_up(self.ny, 128)
        for step in (32, 16, 8):
            if self.rows % step == 0:
                self.step = step
                break
        if self.lanes == 128:
            for step in (128, 80, 64):
                if self.rows % step == 0:
                    self.step = step
                    break

    def scratch(self):
        tall = pltpu.VMEM((self.rows + 2 * G, self.lanes), F32)
        flat = pltpu.VMEM((self.rows, self.lanes), F32)
        return [pltpu.VMEM((7, self.rows, self.lanes), F32), tall, tall, tall, flat, flat]

    def inside(self, start, count, mx, my):
        shape = (count, self.lanes)
        row = iota(shape, 0) + start - self.halo
        lane = iota(shape, 1)
        if not self.split:
            return lane < self.ny
        col = jnp.where(lane >= self.lanes - self.halo, lane - self.lanes, lane)
        row = row + mx * self.bx
        gap = (lane >= self.by + self.halo) & (lane < self.lanes - self.halo)
        col = col + my * self.by
        return (row >= 0) & (row < self.nx) & (col >= 0) & (col < self.ny) & ~gap


def neighbours(win, count, lanes):
    mid = win[G : G + count]
    size = count + 2 * G
    up = pltpu.roll(win, 1, 0)[G : G + count]
    down = pltpu.roll(win, size - 1, 0)[G : G + count]
    before = pltpu.roll(mid, 1, 1)
    after = pltpu.roll(mid, lanes - 1, 1)
    return mid, up, down, before, after


def loop(start, count, step, body):
    for i in range(count // step):
        body(start + i * step)


def setup(level, mx, my, k_ref, s_ref, a_ref, source=None):
    count = level.step

    def body(r):
        mid, up, down, before, after = neighbours(
            k_ref[pl.ds(r, count + 2 * G), :], count, level.lanes
        )
        inside = level.inside(r, count, mx, my)
        if not level.split:
            lane = iota(mid.shape, 1)
            before = jnp.where(lane == 0, 0.0, before)
            after = jnp.where(lane == level.lanes - 1, 0.0, after)
        west, east = 0.5 * (mid + up), 0.5 * (mid + down)
        south, north = 0.5 * (mid + before), 0.5 * (mid + after)
        rows = pl.ds(r, count)
        diag = s_ref[rows, :] + west + east + south + north
        c = jnp.where(inside, OMEGA / diag, 0.0)
        a_ref[0, rows, :] = c * west
        a_ref[1, rows, :] = c * east
        if level.split:
            a_ref[2, rows, :] = c * south
            a_ref[3, rows, :] = c * north
        else:
            a_ref[2, rows, :] = jnp.where(lane == 0, 0.0, c * south)
            a_ref[3, rows, :] = jnp.where(lane == level.ny - 1, 0.0, c * north)
        a_ref[5, rows, :] = c
        a_ref[6, rows, :] = diag * (1.0 / OMEGA)
        if source is not None:
            a_ref[4, rows, :] = c * source[rows_of(r, count), :]

    loop(0, level.rows, count, body)


def rows_of(r, count):
    return pl.ds(r + G, count)


def smooth(level, src, a_ref, put, start=0, total=None):
    count = level.step

    def body(r):
        mid, up, down, before, after = neighbours(
            src[pl.ds(r, count + 2 * G), :], count, level.lanes
        )
        rows = pl.ds(r, count)
        new = (1.0 - OMEGA) * mid + a_ref[4, rows, :]
        new = new + (a_ref[0, rows, :] * up + a_ref[1, rows, :] * down)
        new = new + (a_ref[2, rows, :] * before + a_ref[3, rows, :] * after)
        put(r, rows, mid, new)

    loop(start, level.rows if total is None else total, count, body)


def sweep(level, src, dst, a_ref, start=0, total=None):
    def put(r, rows, mid, new):
        dst[rows_of(r, level.step), :] = new

    smooth(level, src, a_ref, put, start, total)


def residual(level, src, dst, a_ref):
    def put(r, rows, mid, new):
        dst[rows, :] = (new - mid) * a_ref[6, rows, :]

    smooth(level, src, a_ref, put)


def lane_map(fine, coarse, lane):
    half = lane // 2
    if fine.split:
        shift = coarse.lanes - fine.lanes // 2
        half = jnp.where(lane >= fine.lanes - fine.halo, half + shift, half)
    return half


def coarsen(fine, coarse, x):
    shape = (fine.lanes, coarse.lanes)
    cols = ones_where(lane_map(fine, coarse, iota(shape, 0)) == iota(shape, 1))
    shape = (coarse.rows, fine.rows)
    rows = ones_where(iota(shape, 0) == iota(shape, 1) // 2)
    return left(rows, right(x, cols))


def prolong(fine, coarse, mx, my, x):
    shape = (coarse.lanes, fine.lanes)
    lane = iota(shape, 1)
    if fine.split and not coarse.split:
        col = jnp.where(lane >= fine.lanes - fine.halo, lane - fine.lanes, lane)
        gap = (lane >= fine.by + fine.halo) & (lane < fine.lanes - fine.halo)
        target = jnp.where(gap, -2, col + my * fine.by + 2 * coarse.lanes) // 2 - coarse.lanes
        target = jnp.where(gap, -1, target)
    else:
        target = lane_map(fine, coarse, lane)
    cols = ones_where(iota(shape, 0) == target)
    shape = (fine.rows, coarse.rows)
    row = iota(shape, 0)
    if fine.split and not coarse.split:
        row = row - fine.halo + mx * fine.bx
        row = (row + 2 * fine.rows) // 2 - fine.rows
    else:
        row = row // 2
    rows = ones_where(row == iota(shape, 1))
    return left(rows, right(x, cols))


def block_sum(x, first, count, factor, columns, place, lanes):
    shape = (count, x.shape[0])
    row = iota(shape, 1) - first
    rows = ones_where((row >= 0) & (row < count * factor) & ((row + factor) // factor - 1 == iota(shape, 0)))
    shape = (x.shape[1], lanes)
    lane = iota(shape, 0)
    cols = ones_where((lane < columns) & (lane // factor + place == iota(shape, 1)))
    return left(rows, right(x, cols))


def kernel(levels, dx, dy, *refs):
    p_hbm, s_hbm, k_hbm, st_hbm, out_ref = refs[:5]
    ext, strip_l, strip_r, halo_l, halo_r, ga, gb, gca, gcb = refs[5:14]
    held = []
    refs = refs[14:]
    for _ in levels:
        held.append(refs[:6])
        refs = refs[6:]
    load_sem, halo_send, halo_recv, y_send, y_recv, x_send, x_recv = refs

    mx, my = lax.axis_index("gx"), lax.axis_index("gy")
    top = levels[0]
    bx, by = top.bx, top.by
    own = pl.ds(G + HALO, bx)

    loads = []
    for i, ref in enumerate((p_hbm, s_hbm, k_hbm, st_hbm)):
        loads.append(pltpu.make_async_copy(ref, ext.at[i, own, pl.ds(0, by)], load_sem.at[i]))
        loads[-1].start()

    barrier = pltpu.get_barrier_semaphore()
    corners = []
    for sx in (-1, 1):
        for sy in (-1, 1):
            ok = (mx + sx >= 0) & (mx + sx < dx) & (my + sy >= 0) & (my + sy < dy)
            corners.append((sx, sy, ok))
    for d in range(1, dx):
        pl.semaphore_signal(barrier, inc=1, device_id=(lax.rem(mx + d, dx), my), device_id_type=MESH)
    for d in range(1, dy):
        pl.semaphore_signal(barrier, inc=1, device_id=(mx, lax.rem(my + d, dy)), device_id_type=MESH)
    for sx, sy, ok in corners:
        @pl.when(ok)
        def _():
            pl.semaphore_signal(barrier, inc=1, device_id=(mx + sx, my + sy), device_id_type=MESH)

    zero = jnp.zeros((G, top.lanes), F32)
    for i in (0, 2):
        ext[i, 0:G, :] = zero
        ext[i, G + top.rows :, :] = zero
    for level, (a, v, u, k, s, r) in zip(levels, held):
        for ref in (v, u, k):
            ref[0:G, :] = jnp.zeros((G, level.lanes), F32)
            ref[G + level.rows :, :] = jnp.zeros((G, level.lanes), F32)

    for copy in loads:
        copy.wait()

    lane = iota((bx, 128), 1)
    slot = lane // HALO
    for dst, first, at in ((strip_l, 0, 0), (strip_r, by - 128, 128 - HALO)):
        packed = None
        for i in range(4):
            x = ext[i, own, pl.ds(first, 128)]
            turn = (HALO * i - at) % 128
            if turn:
                x = pltpu.roll(x, turn, 1)
            packed = x if packed is None else jnp.where(slot == i, x, packed)
        dst[...] = packed

    corner_count = sum(jnp.where(ok, 1, 0) for _, _, ok in corners)
    pl.semaphore_wait(barrier, dx - 1 + dy - 1 + corner_count)

    halos = []
    n = 0
    for sx in (-1, 0, 1):
        for sy in (-1, 0, 1):
            if sx == 0 and sy == 0:
                continue
            ok = (mx + sx >= 0) & (mx + sx < dx) & (my + sy >= 0) & (my + sy < dy)
            back = (mx - sx >= 0) & (mx - sx < dx) & (my - sy >= 0) & (my - sy < dy)
            if sy == 0:
                first = G + HALO if sx < 0 else G + bx
                there = G + HALO + bx if sx < 0 else G
                src = ext.at[:, pl.ds(first, HALO), pl.ds(0, by)]
                dst = ext.at[:, pl.ds(there, HALO), pl.ds(0, by)]
            else:
                mine, theirs = (strip_l, halo_r) if sy < 0 else (strip_r, halo_l)
                if sx == 0:
                    src, dst = mine, theirs.at[pl.ds(HALO, bx)]
                elif sx < 0:
                    src, dst = mine.at[pl.ds(0, HALO)], theirs.at[pl.ds(HALO + bx, HALO)]
                else:
                    src, dst = mine.at[pl.ds(bx - HALO, HALO)], theirs.at[pl.ds(0, HALO)]
            copy = pltpu.make_async_remote_copy(
                src_ref=src, dst_ref=dst, send_sem=halo_send.at[n], recv_sem=halo_recv.at[n],
                device_id=(mx + sx, my + sy), device_id_type=MESH,
            )
            halos.append((copy, ok, back))
            n += 1
    for copy, ok, _ in halos:
        pl.when(ok)(copy.start)

    whole = levels[LOCAL]
    factor = 1 << LOCAL
    gx_rows, gy_cols = bx // factor, by // factor
    place = my * gy_cols
    sends = []

    def over_gy(buffer, base):
        copies = []
        for d in range(1, dy):
            copies.append(pltpu.make_async_remote_copy(
                src_ref=buffer.at[my], dst_ref=buffer.at[my],
                send_sem=y_send.at[base + d], recv_sem=y_recv.at[base + d],
                device_id=(mx, lax.rem(my + d, dy)), device_id_type=MESH,
            ))
            copies[-1].start()
        sends.extend(copies)
        return copies

    def over_gx(part, base):
        copies = []
        for d in range(1, dx):
            copies.append(pltpu.make_async_remote_copy(
                src_ref=part, dst_ref=part,
                send_sem=x_send.at[base + d], recv_sem=x_recv.at[base + d],
                device_id=(lax.rem(mx + d, dx), my), device_id_type=MESH,
            ))
            copies[-1].start()
        sends.extend(copies)
        return copies

    for i, scale in ((0, 0.5 ** LOCAL), (1, 1.0)):
        x = ext[2 + i, own, pl.ds(0, by)]
        gca[my, i] = scale * block_sum(x, 0, gx_rows, factor, by, place, whole.lanes)
    coef_y = over_gy(gca, 0)

    for copy, _, back in halos:
        pl.when(back)(copy.wait_recv)

    tile = pl.ds(top.lanes - 128, 128)
    lane = iota((HALO, 128), 1)

    @pl.loop(0, top.rows // HALO)
    def _(i):
        r = pl.multiple_of(i * HALO, 8)
        inside = top.inside(r, HALO, mx, my)[:, top.lanes - 128 :]
        lower, upper = halo_l[pl.ds(r, HALO), :], halo_r[pl.ds(r, HALO), :]
        for j in range(4):
            turn_l, turn_r = (128 - HALO - HALO * j) % 128, (-HALO * j) % 128
            x = pltpu.roll(lower, turn_l, 1) if turn_l else lower
            y = pltpu.roll(upper, turn_r, 1) if turn_r else upper
            x = jnp.where(lane < HALO, y, x)
            ext[j, pl.ds(r + G, HALO), tile] = jnp.where(inside, x, 0.0)

    for edge, first in ((mx == 0, G), (mx == dx - 1, G + HALO + bx)):
        @pl.when(edge)
        def _():
            for j in range(4):
                ext[j, pl.ds(first, HALO), pl.ds(0, by)] = jnp.zeros((HALO, by), F32)

    setup(top, mx, my, ext.at[2], ext.at[3, pl.ds(G, top.rows)], held[0][0], ext.at[1])

    for copy in coef_y:
        copy.wait_recv()
    gcb[:, pl.ds(pl.multiple_of(mx * gx_rows, 8), gx_rows), :] = functools.reduce(
        lambda x, y: x + y, [gca[j] for j in range(dy)]
    )
    coef_x = over_gx(gcb.at[:, pl.ds(pl.multiple_of(mx * gx_rows, 8), gx_rows)], 0)

    def inner(level, ref):
        return ref[pl.ds(G, level.rows), :]

    for depth in range(LOCAL):
        level = levels[depth]
        a, v, u, k, s, res = held[depth]
        if depth == 0:
            sweep(level, ext.at[0], v, a)
        else:
            fine = levels[depth - 1]
            fk, fs = (ext.at[2], ext.at[3, pl.ds(G, top.rows)]) if depth == 1 else held[depth - 1][3:5]
            k[pl.ds(G, level.rows), :] = 0.5 * coarsen(fine, level, inner(fine, fk))
            s[...] = coarsen(fine, level, fs[...])
            setup(level, mx, my, k, s, a)
            first = a[5] * coarsen(fine, level, held[depth - 1][5][...])
            a[4] = first
            v[pl.ds(G, level.rows), :] = first
        sweep(level, v, u, a)
        residual(level, u, res, a)

    last = levels[LOCAL - 1]
    ga[my] = block_sum(held[LOCAL - 1][5][...], last.halo, gx_rows, 2, last.by, place, whole.lanes)
    side_y = over_gy(ga, dy)

    for copy in coef_x:
        copy.wait_recv()
    for depth in range(LOCAL, LEVELS):
        level = levels[depth]
        a, v, u, k, s, res = held[depth]
        if depth == LOCAL:
            k[pl.ds(G, level.rows), :] = gcb[0]
            s[...] = gcb[1]
        else:
            fine = levels[depth - 1]
            k[pl.ds(G, level.rows), :] = 0.5 * coarsen(fine, level, inner(fine, held[depth - 1][3]))
            s[...] = coarsen(fine, level, held[depth - 1][4][...])
        setup(level, mx, my, k, s, a)

    for copy in side_y:
        copy.wait_recv()
    part = pl.ds(pl.multiple_of(mx * gx_rows, 8), gx_rows)
    gb[part, :] = functools.reduce(lambda x, y: x + y, [ga[j] for j in range(dy)])
    side_x = over_gx(gb.at[part], dx)
    for copy in side_x:
        copy.wait_recv()

    for depth in range(LOCAL, LEVELS):
        level = levels[depth]
        a, v, u, k, s, res = held[depth]
        side = gb[...] if depth == LOCAL else coarsen(levels[depth - 1], level, held[depth - 1][5][...])
        first = a[5] * side
        a[4] = first
        v[pl.ds(G, level.rows), :] = first
        if depth < LEVELS - 1:
            sweep(level, v, u, a)
            residual(level, u, res, a)
        else:
            for i in range(COARSE_SWEEPS - 1):
                sweep(level, *((v, u) if i % 2 == 0 else (u, v)), a)
            if COARSE_SWEEPS % 2:
                u[...] = v[...]

    for depth in reversed(range(LEVELS - 1)):
        level, below = levels[depth], levels[depth + 1]
        a, v, u, k, s, res = held[depth]
        u[pl.ds(G, level.rows), :] += prolong(level, below, mx, my, inner(below, held[depth + 1][2]))
        if depth:
            sweep(level, u, v, a)
            sweep(level, v, u, a)
        else:
            step = level.step
            sweep(level, u, v, a, HALO - step, bx + 2 * step)

            def put(r, rows, mid, new):
                out_ref[pl.ds(r - HALO, step), :] = new[:, :by]

            smooth(level, v, a, put, HALO, bx)

    for copy, ok, _ in halos:
        pl.when(ok)(copy.wait_send)
    for copy in sends:
        copy.wait_send()


def per_device(nx, ny, pressure, source, conductivity, storage):
    dx, dy = lax.axis_size("gx"), lax.axis_size("gy")
    bx, by = pressure.shape
    levels = [Level(depth, bx, by, nx, ny) for depth in range(LEVELS)]
    top, whole = levels[0], levels[LOCAL]
    rows = bx >> LOCAL
    scratch = [
        pltpu.VMEM((4, top.rows + 2 * G, top.lanes), F32),
        pltpu.VMEM((bx, 128), F32),
        pltpu.VMEM((bx, 128), F32),
        pltpu.VMEM((top.rows, 128), F32),
        pltpu.VMEM((top.rows, 128), F32),
        pltpu.VMEM((dy, rows, whole.lanes), F32),
        pltpu.VMEM((whole.rows, whole.lanes), F32),
        pltpu.VMEM((dy, 2, rows, whole.lanes), F32),
        pltpu.VMEM((2, whole.rows, whole.lanes), F32),
    ]
    for level in levels:
        scratch += level.scratch()
    scratch += [
        pltpu.SemaphoreType.DMA((4,)),
        pltpu.SemaphoreType.DMA((8,)),
        pltpu.SemaphoreType.DMA((8,)),
        pltpu.SemaphoreType.DMA((2 * dy,)),
        pltpu.SemaphoreType.DMA((2 * dy,)),
        pltpu.SemaphoreType.DMA((2 * dx,)),
        pltpu.SemaphoreType.DMA((2 * dx,)),
    ]
    return pl.pallas_call(
        functools.partial(kernel, levels, dx, dy),
        out_shape=jax.ShapeDtypeStruct((bx, by), F32),
        in_specs=[pl.BlockSpec(memory_space=pltpu.HBM)] * 4,
        out_specs=pl.BlockSpec(memory_space=pltpu.VMEM),
        scratch_shapes=scratch,
        compiler_params=pltpu.CompilerParams(
            collective_id=0, has_side_effects=True, vmem_limit_bytes=62 * 2**20
        ),
    )(pressure, source, conductivity, storage)


def solution(mesh):
    placed = (P("gx", "gy"), P("gx", "gy"), P("gx", "gy"), P("gx", "gy"))

    def run(pressure, source, conductivity, storage):
        nx, ny = pressure.shape
        return jax.shard_map(
            functools.partial(per_device, nx, ny),
            mesh=mesh, in_specs=placed, out_specs=P("gx", "gy"), check_vma=False,
        )(pressure, source, conductivity, storage)

    return run
```

```python
import functools

import jax
import jax.numpy as jnp
from jax import lax
from jax.experimental import pallas as pl
from jax.experimental.pallas import tpu as pltpu
from jax.sharding import PartitionSpec as P

LEVELS_SPLIT = 4
LEVELS_MERGED = 2
COARSE_SWEEPS = 8
OMEGA = 0.8

LOCAL = LEVELS_SPLIT - 1
LEVELS = LEVELS_SPLIT + LEVELS_MERGED
HALO = 32
G = 8
MESH = pl.DeviceIdType.MESH
F32 = jnp.float32


def round_up(n, m):
    return -(-n // m) * m


def iota(shape, dim):
    return lax.broadcasted_iota(jnp.int32, shape, dim)


def ones_where(mask):
    return jnp.where(mask, 1.0, 0.0).astype(jnp.bfloat16)


def parts(x):
    high = x.astype(jnp.bfloat16)
    low = (x - high.astype(F32)).astype(jnp.bfloat16)
    return high, low


def dot(a, b):
    return jnp.dot(a, b, preferred_element_type=F32)


def left(matrix, x):
    high, low = parts(x)
    return dot(matrix, high) + dot(matrix, low)


def right(x, matrix):
    high, low = parts(x)
    return dot(high, matrix) + dot(low, matrix)


def put_tiles(ref, rows, x):
    for t in range(x.shape[1] // 128):
        ref[t, rows, :] = x[:, 128 * t : 128 * t + 128]


def pair_rows(ref):
    tiles, rows, _ = ref.shape
    first, second = pl.ds(0, rows // 2, stride=2), pl.ds(1, rows // 2, stride=2)
    return jnp.concatenate([ref[t, first, :] + ref[t, second, :] for t in range(tiles)], axis=1)


def repeat_rows(ref, x):
    tiles, rows, _ = ref.shape
    for t in range(tiles):
        part = x[:, 128 * t : 128 * t + 128]
        ref[t, pl.ds(0, rows // 2, stride=2), :] = part
        ref[t, pl.ds(1, rows // 2, stride=2), :] = part


class Level:
    def __init__(self, depth, bx, by, nx, ny):
        self.depth = depth
        self.split = depth < LOCAL
        self.nx, self.ny = nx >> depth, ny >> depth
        if self.split:
            self.halo = HALO >> depth
            self.bx, self.by = bx >> depth, by >> depth
            self.rows = self.bx + 2 * self.halo
            self.lanes = round_up(self.by + 2 * self.halo, 128)
        else:
            self.halo = 0
            self.bx, self.by = self.nx, self.ny
            self.rows = self.nx
            self.lanes = round_up(self.ny, 128)
        for step in (32, 16, 8):
            if self.rows % step == 0:
                self.step = step
                break
        if self.lanes == 128:
            for step in (128, 80, 64):
                if self.rows % step == 0:
                    self.step = step
                    break

    def scratch(self):
        tall = pltpu.VMEM((self.rows + 2 * G, self.lanes), F32)
        flat = pltpu.VMEM((self.rows, self.lanes), F32)
        tiled = (self.lanes // 128, self.rows, 128)
        return [
            pltpu.VMEM((7, self.rows, self.lanes), F32), tall, tall, tall, flat,
            pltpu.VMEM(tiled, F32), pltpu.VMEM((2, *tiled), F32),
        ]

    def inside(self, start, count, mx, my):
        shape = (count, self.lanes)
        row = iota(shape, 0) + start - self.halo
        lane = iota(shape, 1)
        if not self.split:
            return lane < self.ny
        col = jnp.where(lane >= self.lanes - self.halo, lane - self.lanes, lane)
        row = row + mx * self.bx
        gap = (lane >= self.by + self.halo) & (lane < self.lanes - self.halo)
        col = col + my * self.by
        return (row >= 0) & (row < self.nx) & (col >= 0) & (col < self.ny) & ~gap


def neighbours(win, count, lanes):
    mid = win[G : G + count]
    size = count + 2 * G
    up = pltpu.roll(win, 1, 0)[G : G + count]
    down = pltpu.roll(win, size - 1, 0)[G : G + count]
    before = pltpu.roll(mid, 1, 1)
    after = pltpu.roll(mid, lanes - 1, 1)
    return mid, up, down, before, after


def loop(start, count, step, body):
    for i in range(count // step):
        body(start + i * step)


def setup(level, k_ref, s_ref, a_ref, pairs=None, source=None):
    count = level.step

    def body(r):
        mid, up, down, before, after = neighbours(
            k_ref[pl.ds(r, count + 2 * G), :], count, level.lanes
        )
        inside = mid > 0.0
        if not level.split:
            lane = iota(mid.shape, 1)
            before = jnp.where(lane == 0, 0.0, before)
            after = jnp.where(lane == level.lanes - 1, 0.0, after)
        west, east = 0.5 * (mid + up), 0.5 * (mid + down)
        south, north = 0.5 * (mid + before), 0.5 * (mid + after)
        rows = pl.ds(r, count)
        stored = s_ref[rows, :]
        diag = stored + west + east + south + north
        c = jnp.where(inside, OMEGA / diag, 0.0)
        a_ref[0, rows, :] = c * west
        a_ref[1, rows, :] = c * east
        if level.split:
            a_ref[2, rows, :] = c * south
            a_ref[3, rows, :] = c * north
        else:
            a_ref[2, rows, :] = jnp.where(lane == 0, 0.0, c * south)
            a_ref[3, rows, :] = jnp.where(lane == level.ny - 1, 0.0, c * north)
        a_ref[5, rows, :] = c
        a_ref[6, rows, :] = diag * (1.0 / OMEGA)
        if pairs is not None:
            put_tiles(pairs.at[0], rows, mid)
            put_tiles(pairs.at[1], rows, stored)
        if source is not None:
            a_ref[4, rows, :] = c * source[rows_of(r, count), :]

    loop(0, level.rows, count, body)


def rows_of(r, count):
    return pl.ds(r + G, count)


def smooth(level, src, a_ref, put, start=0, total=None):
    count = level.step

    def body(r):
        mid, up, down, before, after = neighbours(
            src[pl.ds(r, count + 2 * G), :], count, level.lanes
        )
        rows = pl.ds(r, count)
        new = (1.0 - OMEGA) * mid + a_ref[4, rows, :]
        new = new + (a_ref[0, rows, :] * up + a_ref[1, rows, :] * down)
        new = new + (a_ref[2, rows, :] * before + a_ref[3, rows, :] * after)
        put(r, rows, mid, new)

    loop(start, level.rows if total is None else total, count, body)


def sweep(level, src, dst, a_ref, start=0, total=None):
    def put(r, rows, mid, new):
        dst[rows_of(r, level.step), :] = new

    smooth(level, src, a_ref, put, start, total)


def residual(level, src, dst, a_ref):
    def put(r, rows, mid, new):
        put_tiles(dst, rows, (new - mid) * a_ref[6, rows, :])

    smooth(level, src, a_ref, put)


def lane_map(fine, coarse, lane):
    half = lane // 2
    if fine.split:
        shift = coarse.lanes - fine.lanes // 2
        half = jnp.where(lane >= fine.lanes - fine.halo, half + shift, half)
    return half


def matrices(fine, coarse, my):
    shape = (fine.lanes, coarse.lanes)
    lane, there = iota(shape, 0), iota(shape, 1)
    if fine.split and not coarse.split:
        down = (lane < fine.by) & (lane // 2 + my * (fine.by // 2) == there)
    else:
        down = lane_map(fine, coarse, lane) == there
    shape = (coarse.lanes, fine.lanes)
    there, lane = iota(shape, 0), iota(shape, 1)
    if fine.split and not coarse.split:
        col = jnp.where(lane >= fine.lanes - fine.halo, lane - fine.lanes, lane)
        gap = (lane >= fine.by + fine.halo) & (lane < fine.lanes - fine.halo)
        target = (col + my * fine.by + 2 * coarse.lanes) // 2 - coarse.lanes
        up = (there == target) & ~gap
    else:
        up = there == lane_map(fine, coarse, lane)
    return ones_where(down), ones_where(up)


def block_sum(x, first, count, factor, columns, place, lanes):
    shape = (count, x.shape[0])
    row = iota(shape, 1) - first
    rows = ones_where((row >= 0) & (row < count * factor) & ((row + factor) // factor - 1 == iota(shape, 0)))
    shape = (x.shape[1], lanes)
    lane = iota(shape, 0)
    cols = ones_where((lane < columns) & (lane // factor + place == iota(shape, 1)))
    return right(left(rows, x), cols)


def kernel(levels, dx, dy, *refs):
    p_hbm, s_hbm, k_hbm, st_hbm, out_ref = refs[:5]
    ext, strip_l, strip_r, halo_l, halo_r, ga, gb, gca, gcb = refs[5:14]
    held = []
    refs = refs[14:]
    for _ in levels:
        held.append(refs[:7])
        refs = refs[7:]
    downs, ups = refs[: LEVELS - 1], refs[LEVELS - 1 : 2 * LEVELS - 2]
    refs = refs[2 * LEVELS - 2 :]
    stage, out_sem, load_sem, halo_send, halo_recv, y_send, y_recv, x_send, x_recv = refs

    mx, my = lax.axis_index("gx"), lax.axis_index("gy")
    top = levels[0]
    bx, by = top.bx, top.by
    own = pl.ds(G + HALO, bx)

    loads = []
    for i, ref in enumerate((p_hbm, s_hbm, k_hbm, st_hbm)):
        loads.append(pltpu.make_async_copy(ref, ext.at[i, own, pl.ds(0, by)], load_sem.at[i]))
        loads[-1].start()

    barrier = pltpu.get_barrier_semaphore()
    corners = []
    for sx in (-1, 1):
        for sy in (-1, 1):
            ok = (mx + sx >= 0) & (mx + sx < dx) & (my + sy >= 0) & (my + sy < dy)
            corners.append((sx, sy, ok))
    for d in range(1, dx):
        pl.semaphore_signal(barrier, inc=1, device_id=(lax.rem(mx + d, dx), my), device_id_type=MESH)
    for d in range(1, dy):
        pl.semaphore_signal(barrier, inc=1, device_id=(mx, lax.rem(my + d, dy)), device_id_type=MESH)
    for sx, sy, ok in corners:
        @pl.when(ok)
        def _():
            pl.semaphore_signal(barrier, inc=1, device_id=(mx + sx, my + sy), device_id_type=MESH)

    zero = jnp.zeros((G, top.lanes), F32)
    for i in (0, 2):
        ext[i, 0:G, :] = zero
        ext[i, G + top.rows :, :] = zero
    for level, (a, v, u, k, s, r, c) in zip(levels, held):
        for ref in (v, u, k):
            ref[0:G, :] = jnp.zeros((G, level.lanes), F32)
            ref[G + level.rows :, :] = jnp.zeros((G, level.lanes), F32)

    for copy in loads:
        copy.wait()

    lane = iota((bx, 128), 1)
    slot = lane // HALO
    for dst, first, at in ((strip_l, 0, 0), (strip_r, by - 128, 128 - HALO)):
        packed = None
        for i in range(4):
            x = ext[i, own, pl.ds(first, 128)]
            turn = (HALO * i - at) % 128
            if turn:
                x = pltpu.roll(x, turn, 1)
            packed = x if packed is None else jnp.where(slot == i, x, packed)
        dst[...] = packed

    corner_count = sum(jnp.where(ok, 1, 0) for _, _, ok in corners)
    pl.semaphore_wait(barrier, dx - 1 + dy - 1 + corner_count)

    halos = []
    n = 0
    for sx in (-1, 0, 1):
        for sy in (-1, 0, 1):
            if sx == 0 and sy == 0:
                continue
            ok = (mx + sx >= 0) & (mx + sx < dx) & (my + sy >= 0) & (my + sy < dy)
            back = (mx - sx >= 0) & (mx - sx < dx) & (my - sy >= 0) & (my - sy < dy)
            if sy == 0:
                first = G + HALO if sx < 0 else G + bx
                there = G + HALO + bx if sx < 0 else G
                src = ext.at[:, pl.ds(first, HALO), pl.ds(0, by)]
                dst = ext.at[:, pl.ds(there, HALO), pl.ds(0, by)]
            else:
                mine, theirs = (strip_l, halo_r) if sy < 0 else (strip_r, halo_l)
                if sx == 0:
                    src, dst = mine, theirs.at[pl.ds(HALO, bx)]
                elif sx < 0:
                    src, dst = mine.at[pl.ds(0, HALO)], theirs.at[pl.ds(HALO + bx, HALO)]
                else:
                    src, dst = mine.at[pl.ds(bx - HALO, HALO)], theirs.at[pl.ds(0, HALO)]
            copy = pltpu.make_async_remote_copy(
                src_ref=src, dst_ref=dst, send_sem=halo_send.at[n], recv_sem=halo_recv.at[n],
                device_id=(mx + sx, my + sy), device_id_type=MESH,
            )
            halos.append((copy, ok, back))
            n += 1
    for copy, ok, _ in halos:
        pl.when(ok)(copy.start)

    whole = levels[LOCAL]
    factor = 1 << LOCAL
    gx_rows, gy_cols = bx // factor, by // factor
    place = my * gy_cols
    sends = []

    def over_gy(buffer, base):
        copies = []
        for d in range(1, dy):
            copies.append(pltpu.make_async_remote_copy(
                src_ref=buffer.at[my], dst_ref=buffer.at[my],
                send_sem=y_send.at[base + d], recv_sem=y_recv.at[base + d],
                device_id=(mx, lax.rem(my + d, dy)), device_id_type=MESH,
            ))
            copies[-1].start()
        sends.extend(copies)
        return copies

    def over_gx(part, base):
        copies = []
        for d in range(1, dx):
            copies.append(pltpu.make_async_remote_copy(
                src_ref=part, dst_ref=part,
                send_sem=x_send.at[base + d], recv_sem=x_recv.at[base + d],
                device_id=(lax.rem(mx + d, dx), my), device_id_type=MESH,
            ))
            copies[-1].start()
        sends.extend(copies)
        return copies

    for i, scale in ((0, 0.5 ** LOCAL), (1, 1.0)):
        x = ext[2 + i, own, pl.ds(0, by)]
        gca[my, i] = scale * block_sum(x, 0, gx_rows, factor, by, place, whole.lanes)
    coef_y = over_gy(gca, 0)

    for depth in range(LEVELS - 1):
        downs[depth][...], ups[depth][...] = matrices(levels[depth], levels[depth + 1], my)

    for copy, _, back in halos:
        pl.when(back)(copy.wait_recv)

    tile = pl.ds(top.lanes - 128, 128)
    lane = iota((HALO, 128), 1)

    @pl.loop(0, top.rows // HALO)
    def _(i):
        r = pl.multiple_of(i * HALO, 8)
        inside = top.inside(r, HALO, mx, my)[:, top.lanes - 128 :]
        lower, upper = halo_l[pl.ds(r, HALO), :], halo_r[pl.ds(r, HALO), :]
        for j in range(4):
            turn_l, turn_r = (128 - HALO - HALO * j) % 128, (-HALO * j) % 128
            x = pltpu.roll(lower, turn_l, 1) if turn_l else lower
            y = pltpu.roll(upper, turn_r, 1) if turn_r else upper
            x = jnp.where(lane < HALO, y, x)
            ext[j, pl.ds(r + G, HALO), tile] = jnp.where(inside, x, 0.0)

    for edge, first in ((mx == 0, G), (mx == dx - 1, G + HALO + bx)):
        @pl.when(edge)
        def _():
            for j in range(4):
                ext[j, pl.ds(first, HALO), pl.ds(0, by)] = jnp.zeros((HALO, by), F32)

    setup(top, ext.at[2], ext.at[3, pl.ds(G, top.rows)], held[0][0], held[0][6], ext.at[1])

    for copy in coef_y:
        copy.wait_recv()
    gcb[:, pl.ds(pl.multiple_of(mx * gx_rows, 8), gx_rows), :] = functools.reduce(
        lambda x, y: x + y, [gca[j] for j in range(dy)]
    )
    coef_x = over_gx(gcb.at[:, pl.ds(pl.multiple_of(mx * gx_rows, 8), gx_rows)], 0)

    def inner(level, ref):
        return ref[pl.ds(G, level.rows), :]

    def coarse_terms(depth):
        level = levels[depth]
        a, _, _, k, s, _, pairs = held[depth]
        fine = held[depth - 1][6]
        both = jnp.concatenate([pair_rows(fine.at[0]), pair_rows(fine.at[1])], axis=0)
        both = right(both, downs[depth - 1][...])
        k[pl.ds(G, level.rows), :] = 0.5 * both[: level.rows]
        s[...] = both[level.rows :]
        needed = depth != LOCAL - 1 and depth != LEVELS - 1
        setup(level, k, s, a, pairs if needed else None)

    def first_sweep(depth, side):
        level = levels[depth]
        a, v = held[depth][:2]
        first = a[5] * side
        a[4] = first
        v[pl.ds(G, level.rows), :] = first

    for depth in range(LOCAL):
        level = levels[depth]
        a, v, u, k, s, res, _ = held[depth]
        if depth == 0:
            sweep(level, ext.at[0], v, a)
        else:
            coarse_terms(depth)
            first_sweep(depth, right(pair_rows(held[depth - 1][5]), downs[depth - 1][...]))
        sweep(level, v, u, a)
        residual(level, u, res, a)

    last = levels[LOCAL - 1]
    edge = last.halo // 2
    side = right(pair_rows(held[LOCAL - 1][5]), downs[LOCAL - 1][...])
    ga[my] = side[edge : edge + gx_rows]
    side_y = over_gy(ga, dy)

    for copy in coef_x:
        copy.wait_recv()
    a, _, _, k, s, _, pairs = held[LOCAL]
    k[pl.ds(G, whole.rows), :] = gcb[0]
    s[...] = gcb[1]
    setup(whole, k, s, a, pairs)

    for copy in side_y:
        copy.wait_recv()
    part = pl.ds(pl.multiple_of(mx * gx_rows, 8), gx_rows)
    gb[part, :] = functools.reduce(lambda x, y: x + y, [ga[j] for j in range(dy)])
    side_x = over_gx(gb.at[part], dx)

    for depth in range(LOCAL + 1, LEVELS):
        coarse_terms(depth)

    for copy in side_x:
        copy.wait_recv()

    for depth in range(LOCAL, LEVELS):
        level = levels[depth]
        a, v, u, k, s, res, _ = held[depth]
        if depth == LOCAL:
            first_sweep(depth, gb[...])
        else:
            first_sweep(depth, right(pair_rows(held[depth - 1][5]), downs[depth - 1][...]))
        if depth < LEVELS - 1:
            sweep(level, v, u, a)
            residual(level, u, res, a)
        else:
            for i in range(COARSE_SWEEPS - 1):
                sweep(level, *((v, u) if i % 2 == 0 else (u, v)), a)
            if COARSE_SWEEPS % 2:
                u[...] = v[...]

    for depth in reversed(range(LEVELS - 1)):
        level, below = levels[depth], levels[depth + 1]
        a, v, u, k, s, res, _ = held[depth]
        error = held[depth + 1][2]
        if depth == LOCAL - 1:
            window = error[pl.ds(pl.multiple_of(mx * gx_rows, 8), gx_rows + 2 * G), :]
            wide = right(window, ups[depth][...])[G - edge : G + gx_rows + edge]
        else:
            wide = right(error[pl.ds(G, below.rows), :], ups[depth][...])
        repeat_rows(res, wide)
        tiles = [res[t] for t in range(level.lanes // 128)]
        u[pl.ds(G, level.rows), :] += jnp.concatenate(tiles, axis=1)
        if depth:
            sweep(level, u, v, a)
            sweep(level, v, u, a)
        else:
            step = level.step
            sweep(level, u, v, a, HALO - step, bx + 2 * step)

            def put(r, rows, mid, new):
                stage[pl.ds(r - HALO, step), :] = new[:, :by]

            half = bx // 2
            results = []
            for i in range(2):
                smooth(level, v, a, put, HALO + i * half, half)
                part = pl.ds(i * half, half)
                results.append(pltpu.make_async_copy(stage.at[part], out_ref.at[part], out_sem.at[i]))
                results[-1].start()

    for copy, ok, _ in halos:
        pl.when(ok)(copy.wait_send)
    for copy in sends:
        copy.wait_send()
    for copy in results:
        copy.wait()


def per_device(nx, ny, pressure, source, conductivity, storage):
    dx, dy = lax.axis_size("gx"), lax.axis_size("gy")
    bx, by = pressure.shape
    levels = [Level(depth, bx, by, nx, ny) for depth in range(LEVELS)]
    top, whole = levels[0], levels[LOCAL]
    rows = bx >> LOCAL
    scratch = [
        pltpu.VMEM((4, top.rows + 2 * G, top.lanes), F32),
        pltpu.VMEM((bx, 128), F32),
        pltpu.VMEM((bx, 128), F32),
        pltpu.VMEM((top.rows, 128), F32),
        pltpu.VMEM((top.rows, 128), F32),
        pltpu.VMEM((dy, rows, whole.lanes), F32),
        pltpu.VMEM((whole.rows, whole.lanes), F32),
        pltpu.VMEM((dy, 2, rows, whole.lanes), F32),
        pltpu.VMEM((2, whole.rows, whole.lanes), F32),
    ]
    for level in levels:
        scratch += level.scratch()
    pairs = list(zip(levels, levels[1:]))
    scratch += [pltpu.VMEM((fine.lanes, coarse.lanes), jnp.bfloat16) for fine, coarse in pairs]
    scratch += [pltpu.VMEM((coarse.lanes, fine.lanes), jnp.bfloat16) for fine, coarse in pairs]
    scratch += [
        pltpu.VMEM((bx, by), F32),
        pltpu.SemaphoreType.DMA((2,)),
        pltpu.SemaphoreType.DMA((4,)),
        pltpu.SemaphoreType.DMA((8,)),
        pltpu.SemaphoreType.DMA((8,)),
        pltpu.SemaphoreType.DMA((2 * dy,)),
        pltpu.SemaphoreType.DMA((2 * dy,)),
        pltpu.SemaphoreType.DMA((2 * dx,)),
        pltpu.SemaphoreType.DMA((2 * dx,)),
    ]
    return pl.pallas_call(
        functools.partial(kernel, levels, dx, dy),
        out_shape=jax.ShapeDtypeStruct((bx, by), F32),
        in_specs=[pl.BlockSpec(memory_space=pltpu.HBM)] * 4,
        out_specs=pl.BlockSpec(memory_space=pltpu.HBM),
        scratch_shapes=scratch,
        compiler_params=pltpu.CompilerParams(
            collective_id=0, has_side_effects=True, vmem_limit_bytes=62 * 2**20
        ),
    )(pressure, source, conductivity, storage)


def solution(mesh):
    placed = (P("gx", "gy"), P("gx", "gy"), P("gx", "gy"), P("gx", "gy"))

    def run(pressure, source, conductivity, storage):
        nx, ny = pressure.shape
        return jax.shard_map(
            functools.partial(per_device, nx, ny),
            mesh=mesh, in_specs=placed, out_specs=P("gx", "gy"), check_vma=False,
        )(pressure, source, conductivity, storage)

    return run
```

```python
import functools

import jax
import jax.numpy as jnp
from jax import lax
from jax.experimental import pallas as pl
from jax.experimental.pallas import tpu as pltpu
from jax.sharding import PartitionSpec as P

LEVELS_SPLIT = 4
LEVELS_MERGED = 2
COARSE_SWEEPS = 8
OMEGA = 0.8

LOCAL = LEVELS_SPLIT - 1
LEVELS = LEVELS_SPLIT + LEVELS_MERGED
HALOS = (8, 16, 8)
G = 8
MESH = pl.DeviceIdType.MESH
F32 = jnp.float32


def round_up(n, m):
    return -(-n // m) * m


def iota(shape, dim):
    return lax.broadcasted_iota(jnp.int32, shape, dim)


def ones_where(mask):
    return jnp.where(mask, 1.0, 0.0).astype(jnp.bfloat16)


def parts(x):
    high = x.astype(jnp.bfloat16)
    low = (x - high.astype(F32)).astype(jnp.bfloat16)
    return high, low


def dot(a, b):
    return jnp.dot(a, b, preferred_element_type=F32)


def left(matrix, x):
    high, low = parts(x)
    return dot(matrix, high) + dot(matrix, low)


def right(x, matrix):
    high, low = parts(x)
    return dot(high, matrix) + dot(low, matrix)


def put_tiles(ref, rows, x):
    for t in range(x.shape[1] // 128):
        ref[t, rows, :] = x[:, 128 * t : 128 * t + 128]


def pair_rows(ref):
    tiles, rows, _ = ref.shape
    first, second = pl.ds(0, rows // 2, stride=2), pl.ds(1, rows // 2, stride=2)
    return jnp.concatenate([ref[t, first, :] + ref[t, second, :] for t in range(tiles)], axis=1)


def repeat_rows(ref, x):
    tiles, rows, _ = ref.shape
    for t in range(tiles):
        part = x[:, 128 * t : 128 * t + 128]
        ref[t, pl.ds(0, rows // 2, stride=2), :] = part
        ref[t, pl.ds(1, rows // 2, stride=2), :] = part


class Level:
    def __init__(self, depth, bx, by, nx, ny):
        self.depth = depth
        self.split = depth < LOCAL
        self.nx, self.ny = nx >> depth, ny >> depth
        if self.split:
            self.halo = HALOS[depth]
            self.bx, self.by = bx >> depth, by >> depth
            self.rows = self.bx + 2 * self.halo
            self.lanes = round_up(self.by + 2 * self.halo, 128)
        else:
            self.halo = 0
            self.bx, self.by = self.nx, self.ny
            self.rows = self.nx
            self.lanes = round_up(self.ny, 128)
        self.step = 32 if self.lanes > 128 else 128

    def scratch(self):
        tall = pltpu.VMEM((self.rows + 2 * G, self.lanes), F32)
        flat = pltpu.VMEM((self.rows, self.lanes), F32)
        tiled = (self.lanes // 128, self.rows, 128)
        return [
            pltpu.VMEM((7, self.rows, self.lanes), F32), tall, tall, tall, flat,
            pltpu.VMEM(tiled, F32), pltpu.VMEM((2, *tiled), F32),
        ]


def neighbours(win, count, lanes):
    mid = win[G : G + count]
    size = count + 2 * G
    up = pltpu.roll(win, 1, 0)[G : G + count]
    down = pltpu.roll(win, size - 1, 0)[G : G + count]
    before = pltpu.roll(mid, 1, 1)
    after = pltpu.roll(mid, lanes - 1, 1)
    return mid, up, down, before, after


def loop(start, count, step, body):
    for r in range(0, count, step):
        body(start + r, min(step, count - r))


def setup(level, k_ref, s_ref, a_ref, pairs=None, source=None):
    def body(r, count):
        mid, up, down, before, after = neighbours(
            k_ref[pl.ds(r, count + 2 * G), :], count, level.lanes
        )
        inside = mid > 0.0
        if not level.split:
            lane = iota(mid.shape, 1)
            before = jnp.where(lane == 0, 0.0, before)
            after = jnp.where(lane == level.lanes - 1, 0.0, after)
        west, east = 0.5 * (mid + up), 0.5 * (mid + down)
        south, north = 0.5 * (mid + before), 0.5 * (mid + after)
        rows = pl.ds(r, count)
        stored = s_ref[rows, :]
        diag = stored + west + east + south + north
        c = jnp.where(inside, OMEGA / diag, 0.0)
        a_ref[0, rows, :] = c * west
        a_ref[1, rows, :] = c * east
        if level.split:
            a_ref[2, rows, :] = c * south
            a_ref[3, rows, :] = c * north
        else:
            a_ref[2, rows, :] = jnp.where(lane == 0, 0.0, c * south)
            a_ref[3, rows, :] = jnp.where(lane == level.ny - 1, 0.0, c * north)
        a_ref[5, rows, :] = c
        a_ref[6, rows, :] = diag * (1.0 / OMEGA)
        if pairs is not None:
            put_tiles(pairs.at[0], rows, mid)
            put_tiles(pairs.at[1], rows, stored)
        if source is not None:
            a_ref[4, rows, :] = c * source[rows_of(r, count), :]

    loop(0, level.rows, level.step, body)


def rows_of(r, count):
    return pl.ds(r + G, count)


def smooth(level, src, a_ref, put, start=0, total=None):
    def body(r, count):
        mid, up, down, before, after = neighbours(
            src[pl.ds(r, count + 2 * G), :], count, level.lanes
        )
        rows = pl.ds(r, count)
        new = (1.0 - OMEGA) * mid + a_ref[4, rows, :]
        new = new + (a_ref[0, rows, :] * up + a_ref[1, rows, :] * down)
        new = new + (a_ref[2, rows, :] * before + a_ref[3, rows, :] * after)
        put(r, rows, mid, new)

    loop(start, level.rows if total is None else total, level.step, body)


def sweep(level, src, dst, a_ref, start=0, total=None):
    def put(r, rows, mid, new):
        dst[rows_of(r, rows.size), :] = new

    smooth(level, src, a_ref, put, start, total)


def residual(level, src, dst, a_ref):
    def put(r, rows, mid, new):
        put_tiles(dst, rows, (new - mid) * a_ref[6, rows, :])

    smooth(level, src, a_ref, put)


def residual_own(level, src, dst, a_ref):
    def put(r, rows, mid, new):
        part = (new - mid) * a_ref[6, rows, :]
        put_tiles(dst, pl.ds(r - level.halo, rows.size), part[:, : level.by])

    smooth(level, src, a_ref, put, level.halo, level.bx)


def lane_map(fine, coarse, lane):
    half = lane // 2
    if fine.split:
        shift = coarse.lanes - fine.lanes // 2
        half = jnp.where(lane >= fine.lanes - fine.halo, half + shift, half)
    return half


def matrices(fine, coarse, my):
    shape = (fine.by, coarse.by) if fine.depth == 0 else (fine.lanes, coarse.lanes)
    lane, there = iota(shape, 0), iota(shape, 1)
    if fine.depth == 0:
        down = lane // 2 == there
    elif fine.split and not coarse.split:
        down = (lane < fine.by) & (lane // 2 + my * (fine.by // 2) == there)
    else:
        down = lane_map(fine, coarse, lane) == there
    shape = (coarse.lanes, fine.lanes)
    there, lane = iota(shape, 0), iota(shape, 1)
    if fine.split and not coarse.split:
        col = jnp.where(lane >= fine.lanes - fine.halo, lane - fine.lanes, lane)
        gap = (lane >= fine.by + fine.halo) & (lane < fine.lanes - fine.halo)
        target = (col + my * fine.by + 2 * coarse.lanes) // 2 - coarse.lanes
        up = (there == target) & ~gap
    else:
        up = there == lane_map(fine, coarse, lane)
    return ones_where(down), ones_where(up)


def block_sum(x, count, factor, place):
    shape = (count, x.shape[0])
    rows = ones_where(iota(shape, 1) // factor == iota(shape, 0))
    shape = (x.shape[1], 128)
    cols = ones_where(iota(shape, 0) // factor + place == iota(shape, 1))
    return right(left(rows, x), cols)


class Exchange:
    def __init__(self, ext, scratch, level, here, size):
        self.ext, self.level = ext, level
        self.strips, self.halos = scratch[:2], scratch[2:4]
        self.mx, self.my = here
        self.dx, self.dy = size
        self.count, self.width = ext.shape[0], level.halo
        self.groups = 128 // (self.count * self.width)
        self.rows = level.bx // self.groups
        self.copies = []
        bx, by, w, rows = level.bx, level.by, self.width, self.rows
        for n, (sx, sy) in enumerate((i, j) for i in (-1, 0, 1) for j in (-1, 0, 1) if i or j):
            if sy == 0:
                first = G + w if sx < 0 else G + bx
                there = G + w + bx if sx < 0 else G
                src = ext.at[:, pl.ds(first, w), pl.ds(0, by)]
                dst = ext.at[:, pl.ds(there, w), pl.ds(0, by)]
            else:
                mine, theirs = (self.strips[0], self.halos[1]) if sy < 0 else (self.strips[1], self.halos[0])
                if sx == 0:
                    src, dst = mine, theirs.at[pl.ds(w, rows)]
                elif sx < 0:
                    src, dst = mine.at[pl.ds(0, w)], theirs.at[pl.ds(w + rows, w)]
                else:
                    src, dst = mine.at[pl.ds(rows - w, w)], theirs.at[pl.ds(0, w)]
            copy = pltpu.make_async_remote_copy(
                src_ref=src, dst_ref=dst, send_sem=scratch[4].at[n], recv_sem=scratch[5].at[n],
                device_id=(self.mx + sx, self.my + sy), device_id_type=MESH,
            )
            self.copies.append((copy, self.there(sx, sy), self.there(-sx, -sy)))

    @staticmethod
    def scratch(level, count):
        rows = level.bx * level.halo * count // 128
        strip, halo = pltpu.VMEM((rows, 128), F32), pltpu.VMEM((rows + 2 * level.halo, 128), F32)
        return [strip, strip, halo, halo, pltpu.SemaphoreType.DMA((8,)), pltpu.SemaphoreType.DMA((8,))]

    def there(self, sx, sy):
        x, y = self.mx + sx, self.my + sy
        return (x >= 0) & (x < self.dx) & (y >= 0) & (y < self.dy)

    def pack(self):
        level, w = self.level, self.width
        slot = iota((self.rows, 128), 1) // w
        for strip, first, at in ((self.strips[0], 0, 0), (self.strips[1], level.by - 128, 128 - w)):
            packed = None
            for i in range(self.count * self.groups):
                group, j = divmod(i, self.count)
                x = self.ext[j, pl.ds(G + w + group * self.rows, self.rows), pl.ds(first, 128)]
                turn = (w * i - at) % 128
                if turn:
                    x = pltpu.roll(x, turn, 1)
                packed = x if packed is None else jnp.where(slot == i, x, packed)
            strip[...] = packed

    def start(self):
        for copy, ok, _ in self.copies:
            pl.when(ok)(copy.start)

    def finish(self):
        for copy, _, back in self.copies:
            pl.when(back)(copy.wait_recv)
        level, w, rows = self.level, self.width, self.rows
        tile = pl.ds(level.lanes - 128, 128)
        blocks = [(0, w, self.groups - 1, G), (w + rows, w, 0, G + w + level.bx)]
        blocks += [(w, rows, g, G + w + g * rows) for g in range(self.groups)]
        for first, count, group, there in blocks:
            lower, upper = (ref[pl.ds(first, count), :] for ref in self.halos)
            lane = iota((count, 128), 1)
            right_part = (lane < w) & (self.my < self.dy - 1)
            left_part = (lane >= 128 - w) & (self.my > 0)
            for j in range(self.count):
                at = (group * self.count + j) * w
                turn_l, turn_r = (128 - w - at) % 128, -at % 128
                x = pltpu.roll(lower, turn_l, 1) if turn_l else lower
                y = pltpu.roll(upper, turn_r, 1) if turn_r else upper
                x = jnp.where(right_part, y, jnp.where(left_part, x, 0.0))
                self.ext[j, pl.ds(there, count), tile] = x
        for edge, first in ((self.mx == 0, G), (self.mx == self.dx - 1, G + w + level.bx)):
            @pl.when(edge)
            def _():
                self.ext[:, pl.ds(first, w), :] = jnp.zeros((self.count, w, level.lanes), F32)

    def drain(self):
        for copy, ok, _ in self.copies:
            pl.when(ok)(copy.wait_send)


def kernel(levels, dx, dy, *refs):
    p_hbm, s_hbm, k_hbm, st_hbm, out_ref = refs[:5]
    ext, ext_coef, ext_side, own_res, own_pairs, ga, gb, gca, gcb = refs[5:14]
    refs = refs[14:]
    ex_scratch, refs = [refs[:6], refs[6:12], refs[12:18]], refs[18:]
    held = []
    for _ in levels:
        held.append(list(refs[:7]))
        refs = refs[7:]
    downs, ups = refs[: LEVELS - 1], refs[LEVELS - 1 : 2 * LEVELS - 2]
    refs = refs[2 * LEVELS - 2 :]
    stage, out_sem, load_sem, y_send, y_recv, x_send, x_recv = refs

    mx, my = lax.axis_index("gx"), lax.axis_index("gy")
    top, second = levels[:2]
    bx, by = top.bx, top.by
    own = pl.ds(G + top.halo, bx)
    held[1][3], held[1][4] = ext_coef.at[0], ext_coef.at[1, pl.ds(G, second.rows)]

    loads, tiled_loads = [], []
    for i, ref in enumerate((p_hbm, s_hbm, k_hbm, st_hbm)):
        loads.append(pltpu.make_async_copy(ref, ext.at[i, own, pl.ds(0, by)], load_sem.at[i]))
        loads[-1].start()
    for i, ref in enumerate((k_hbm, st_hbm)):
        for t in range(by // 128):
            tiled_loads.append(pltpu.make_async_copy(
                ref.at[:, pl.ds(128 * t, 128)], own_pairs.at[i, t], load_sem.at[4 + i * (by // 128) + t]
            ))
            tiled_loads[-1].start()

    halo = Exchange(ext, ex_scratch[0], top, (mx, my), (dx, dy))
    halo_coef = Exchange(ext_coef, ex_scratch[1], second, (mx, my), (dx, dy))
    halo_side = Exchange(ext_side, ex_scratch[2], second, (mx, my), (dx, dy))

    barrier = pltpu.get_barrier_semaphore()
    for d in range(1, dx):
        pl.semaphore_signal(barrier, inc=1, device_id=(lax.rem(mx + d, dx), my), device_id_type=MESH)
    for d in range(1, dy):
        pl.semaphore_signal(barrier, inc=1, device_id=(mx, lax.rem(my + d, dy)), device_id_type=MESH)
    signals = dx - 1 + dy - 1
    for sx in (-1, 1):
        for sy in (-1, 1):
            ok = halo.there(sx, sy)
            signals = signals + jnp.where(ok, 1, 0)
            @pl.when(ok)
            def _():
                pl.semaphore_signal(barrier, inc=1, device_id=(mx + sx, my + sy), device_id_type=MESH)

    for ref, level in ((ext.at[0], top), (ext.at[2], top), (ext_coef.at[0], second)):
        ref[0:G, :] = jnp.zeros((G, level.lanes), F32)
        ref[G + level.rows :, :] = jnp.zeros((G, level.lanes), F32)
    for level, (a, v, u, k, s, r, c) in zip(levels, held):
        for ref in (v, u, k):
            ref[0:G, :] = jnp.zeros((G, level.lanes), F32)
            ref[G + level.rows :, :] = jnp.zeros((G, level.lanes), F32)
    downs[0][...], ups[0][...] = matrices(top, second, my)

    for copy in loads:
        copy.wait()
    halo.pack()
    pl.semaphore_wait(barrier, signals)
    halo.start()

    for copy in tiled_loads:
        copy.wait()
    half = bx // 2
    own_second = pl.ds(G + second.halo, half)
    both = jnp.concatenate([pair_rows(own_pairs.at[0]), pair_rows(own_pairs.at[1])], axis=0)
    both = right(both, downs[0][...])
    near_k, near_s = 0.5 * both[:half], both[half:]
    ext_coef[0, own_second, 0 : by // 2] = near_k
    ext_coef[1, own_second, 0 : by // 2] = near_s

    whole = levels[LOCAL]
    factor = 1 << LOCAL
    gx_rows, gy_cols = bx // factor, by // factor
    sends = []

    def send(src, dst, sems, n, target):
        copy = pltpu.make_async_remote_copy(
            src_ref=src, dst_ref=dst, send_sem=sems[0].at[n], recv_sem=sems[1].at[n],
            device_id=target, device_id_type=MESH,
        )
        copy.start()
        sends.append(copy)
        return copy

    def over_gy(buffer, base):
        return [
            send(buffer.at[my], buffer.at[my], (y_send, y_recv), base + d, (mx, lax.rem(my + d, dy)))
            for d in range(1, dy)
        ]

    def strip_of(row):
        return pl.ds(pl.multiple_of(row * gx_rows, 8), gx_rows)

    far_k = 0.5 ** (LOCAL - 1) * block_sum(near_k, gx_rows, factor // 2, 0)
    gca[my] = far_k + block_sum(near_s, gx_rows, factor // 2, gy_cols)
    coef_y = over_gy(gca, 0)
    halo_coef.pack()
    halo_coef.start()

    for depth in range(1, LEVELS - 1):
        downs[depth][...], ups[depth][...] = matrices(levels[depth], levels[depth + 1], my)

    halo.finish()
    setup(top, ext.at[2], ext.at[3, pl.ds(G, top.rows)], held[0][0], None, ext.at[1])

    for copy in coef_y:
        copy.wait_recv()
    lane = iota((gx_rows, whole.lanes), 1)
    for i in range(2):
        merged = jnp.zeros((gx_rows, whole.lanes), F32)
        for j in range(dy):
            first = gy_cols * j
            x = jnp.concatenate([gca[j]] * (whole.lanes // 128), axis=1)
            turn = (first - gy_cols * i) % whole.lanes
            x = pltpu.roll(x, turn, 1) if turn else x
            merged = jnp.where((lane >= first) & (lane < first + gy_cols), x, merged)
        gcb[i, strip_of(mx), :] = merged
    mine = gcb.at[:, strip_of(mx)]
    coef_x = [
        send(mine, mine, (x_send, x_recv), d, (lax.rem(mx + d, dx), my)) for d in range(2, dx, 2)
    ]

    def coarse_terms(depth):
        level = levels[depth]
        a, _, _, k, s, _, pairs = held[depth]
        fine = held[depth - 1][6]
        both = jnp.concatenate([pair_rows(fine.at[0]), pair_rows(fine.at[1])], axis=0)
        both = right(both, downs[depth - 1][...])
        k[pl.ds(G, level.rows), :] = 0.5 * both[: level.rows]
        s[...] = both[level.rows :]
        needed = depth != LOCAL - 1 and depth != LEVELS - 1
        setup(level, k, s, a, pairs if needed else None)

    def first_sweep(depth, side):
        level = levels[depth]
        a, v = held[depth][:2]
        first = a[5] * side
        a[4] = first
        v[pl.ds(G, level.rows), :] = first

    sweep(top, ext.at[0], held[0][1], held[0][0])
    sweep(top, held[0][1], held[0][2], held[0][0])
    residual_own(top, held[0][2], own_res, held[0][0])
    ext_side[0, own_second, 0 : by // 2] = right(pair_rows(own_res), downs[0][...])
    halo_side.pack()
    halo_side.start()

    halo_coef.finish()
    setup(second, held[1][3], held[1][4], held[1][0], held[1][6])
    for depth in range(2, LOCAL):
        coarse_terms(depth)
    for copy in coef_x:
        copy.wait_recv()
    core = lax.rem(mx, 2)
    coef_x = []
    for chip in range(dx // 2):
        part = gcb.at[:, strip_of(2 * chip + core)]
        coef_x.append(send(part, part, (x_send, x_recv), 2 * dx + chip, (mx + 1 - 2 * core, my)))

    halo_side.finish()
    for depth in range(1, LOCAL):
        level = levels[depth]
        a, v, u, k, s, res, _ = held[depth]
        if depth == 1:
            first_sweep(depth, ext_side[0, pl.ds(G, level.rows), :])
        else:
            first_sweep(depth, right(pair_rows(held[depth - 1][5]), downs[depth - 1][...]))
        sweep(level, v, u, a)
        residual(level, u, res, a)

    last = levels[LOCAL - 1]
    edge = last.halo // 2
    side = right(pair_rows(held[LOCAL - 1][5]), downs[LOCAL - 1][...])
    ga[my] = side[edge : edge + gx_rows]
    side_y = over_gy(ga, dy)

    for copy in coef_x:
        copy.wait_recv()
    a, _, _, k, s, _, pairs = held[LOCAL]
    k[pl.ds(G, whole.rows), :] = gcb[0]
    s[...] = gcb[1]
    setup(whole, k, s, a, pairs)

    for copy in side_y:
        copy.wait_recv()
    gb[strip_of(mx), :] = functools.reduce(lambda x, y: x + y, [ga[j] for j in range(dy)])
    mine = gb.at[strip_of(mx)]
    side_x = [
        send(mine, mine, (x_send, x_recv), dx + d, (lax.rem(mx + d, dx), my)) for d in range(1, dx)
    ]

    for depth in range(LOCAL + 1, LEVELS):
        coarse_terms(depth)

    for copy in side_x:
        copy.wait_recv()

    for depth in range(LOCAL, LEVELS):
        level = levels[depth]
        a, v, u, k, s, res, _ = held[depth]
        if depth == LOCAL:
            first_sweep(depth, gb[...])
        else:
            first_sweep(depth, right(pair_rows(held[depth - 1][5]), downs[depth - 1][...]))
        if depth < LEVELS - 1:
            sweep(level, v, u, a)
            residual(level, u, res, a)
        else:
            for i in range(COARSE_SWEEPS - 1):
                sweep(level, *((v, u) if i % 2 == 0 else (u, v)), a)
            if COARSE_SWEEPS % 2:
                u[...] = v[...]

    for depth in reversed(range(LEVELS - 1)):
        level, below = levels[depth], levels[depth + 1]
        a, v, u, k, s, res, _ = held[depth]
        error = held[depth + 1][2]
        if depth == LOCAL - 1:
            window = error[pl.ds(pl.multiple_of(mx * gx_rows, 8), gx_rows + 2 * G), :]
            wide = right(window, ups[depth][...])[G - edge : G + gx_rows + edge]
        else:
            skip = below.halo - level.halo // 2
            wide = right(error[pl.ds(G + skip, below.rows - 2 * skip), :], ups[depth][...])
        repeat_rows(res, wide)
        tiles = [res[t] for t in range(level.lanes // 128)]
        u[pl.ds(G, level.rows), :] += jnp.concatenate(tiles, axis=1)
        if depth:
            sweep(level, u, v, a)
            sweep(level, v, u, a)
        else:
            sweep(level, u, v, a)

            def put(r, rows, mid, new):
                stage[pl.ds(r - level.halo, rows.size), :] = new[:, :by]

            half = bx // 2
            results = []
            for i in range(2):
                smooth(level, v, a, put, level.halo + i * half, half)
                part = pl.ds(i * half, half)
                results.append(pltpu.make_async_copy(stage.at[part], out_ref.at[part], out_sem.at[i]))
                results[-1].start()

    for exchange in (halo, halo_coef, halo_side):
        exchange.drain()
    for copy in sends:
        copy.wait_send()
    for copy in results:
        copy.wait()


def per_device(nx, ny, pressure, source, conductivity, storage):
    dx, dy = lax.axis_size("gx"), lax.axis_size("gy")
    bx, by = pressure.shape
    levels = [Level(depth, bx, by, nx, ny) for depth in range(LEVELS)]
    top, second, whole = levels[0], levels[1], levels[LOCAL]
    rows, tiles = bx >> LOCAL, by // 128
    scratch = [
        pltpu.VMEM((4, top.rows + 2 * G, top.lanes), F32),
        pltpu.VMEM((2, second.rows + 2 * G, second.lanes), F32),
        pltpu.VMEM((1, second.rows + 2 * G, second.lanes), F32),
        pltpu.VMEM((tiles, bx, 128), F32),
        pltpu.VMEM((2, tiles, bx, 128), F32),
        pltpu.VMEM((dy, rows, whole.lanes), F32),
        pltpu.VMEM((whole.rows, whole.lanes), F32),
        pltpu.VMEM((dy, rows, 128), F32),
        pltpu.VMEM((2, whole.rows, whole.lanes), F32),
    ]
    for level, count in ((top, 4), (second, 2), (second, 1)):
        scratch += Exchange.scratch(level, count)
    for level in levels:
        scratch += level.scratch()
    pairs = list(zip(levels, levels[1:]))
    scratch += [
        pltpu.VMEM((fine.lanes, coarse.lanes) if fine.depth else (by, by // 2), jnp.bfloat16)
        for fine, coarse in pairs
    ]
    scratch += [pltpu.VMEM((coarse.lanes, fine.lanes), jnp.bfloat16) for fine, coarse in pairs]
    scratch += [
        pltpu.VMEM((bx, by), F32),
        pltpu.SemaphoreType.DMA((2,)),
        pltpu.SemaphoreType.DMA((4 + 2 * tiles,)),
        pltpu.SemaphoreType.DMA((2 * dy,)),
        pltpu.SemaphoreType.DMA((2 * dy,)),
        pltpu.SemaphoreType.DMA((3 * dx,)),
        pltpu.SemaphoreType.DMA((3 * dx,)),
    ]
    return pl.pallas_call(
        functools.partial(kernel, levels, dx, dy),
        out_shape=jax.ShapeDtypeStruct((bx, by), F32),
        in_specs=[pl.BlockSpec(memory_space=pltpu.HBM)] * 4,
        out_specs=pl.BlockSpec(memory_space=pltpu.HBM),
        scratch_shapes=scratch,
        compiler_params=pltpu.CompilerParams(
            collective_id=0, has_side_effects=True, vmem_limit_bytes=62 * 2**20
        ),
    )(pressure, source, conductivity, storage)


def solution(mesh):
    placed = (P("gx", "gy"), P("gx", "gy"), P("gx", "gy"), P("gx", "gy"))

    def run(pressure, source, conductivity, storage):
        nx, ny = pressure.shape
        return jax.shard_map(
            functools.partial(per_device, nx, ny),
            mesh=mesh, in_specs=placed, out_specs=P("gx", "gy"), check_vma=False,
        )(pressure, source, conductivity, storage)

    return run
```

```python
import functools

import jax
import jax.numpy as jnp
from jax import lax
from jax.experimental import pallas as pl
from jax.experimental.pallas import tpu as pltpu
from jax.sharding import PartitionSpec as P

LEVELS_SPLIT = 4
LEVELS_MERGED = 2
COARSE_SWEEPS = 8
OMEGA = 0.8

LOCAL = LEVELS_SPLIT - 1
LEVELS = LEVELS_SPLIT + LEVELS_MERGED
HALOS = (8, 16, 8)
G = 8
MESH = pl.DeviceIdType.MESH
F32 = jnp.float32


def round_up(n, m):
    return -(-n // m) * m


def iota(shape, dim):
    return lax.broadcasted_iota(jnp.int32, shape, dim)


def ones_where(mask):
    return jnp.where(mask, 1.0, 0.0).astype(jnp.bfloat16)


def parts(x):
    high = x.astype(jnp.bfloat16)
    low = (x - high.astype(F32)).astype(jnp.bfloat16)
    return high, low


def dot(a, b):
    return jnp.dot(a, b, preferred_element_type=F32)


def left(matrix, x):
    high, low = parts(x)
    return dot(matrix, high) + dot(matrix, low)


def right(x, matrix):
    high, low = parts(x)
    return dot(high, matrix) + dot(low, matrix)


def put_tiles(ref, rows, x):
    for t in range(x.shape[1] // 128):
        ref[t, rows, :] = x[:, 128 * t : 128 * t + 128]


def pair_rows(ref):
    tiles, rows, _ = ref.shape
    first, second = pl.ds(0, rows // 2, stride=2), pl.ds(1, rows // 2, stride=2)
    return jnp.concatenate([ref[t, first, :] + ref[t, second, :] for t in range(tiles)], axis=1)


def repeat_rows(ref, x):
    tiles, rows, _ = ref.shape
    for t in range(tiles):
        part = x[:, 128 * t : 128 * t + 128]
        ref[t, pl.ds(0, rows // 2, stride=2), :] = part
        ref[t, pl.ds(1, rows // 2, stride=2), :] = part


class Level:
    def __init__(self, depth, bx, by, nx, ny):
        self.depth = depth
        self.split = depth < LOCAL
        self.nx, self.ny = nx >> depth, ny >> depth
        if self.split:
            self.halo = HALOS[depth]
            self.bx, self.by = bx >> depth, by >> depth
            self.rows = self.bx + 2 * self.halo
            self.lanes = round_up(self.by + 2 * self.halo, 128)
        else:
            self.halo = 0
            self.bx, self.by = self.nx, self.ny
            self.rows = self.nx
            self.lanes = round_up(self.ny, 128)
        self.step = 32 if self.lanes > 128 else 128

    def scratch(self):
        tall = pltpu.VMEM((self.rows + 2 * G, self.lanes), F32)
        flat = pltpu.VMEM((self.rows, self.lanes), F32)
        tiled = (self.lanes // 128, self.rows, 128)
        return [
            pltpu.VMEM((7, self.rows, self.lanes), F32), tall, tall, tall, flat,
            pltpu.VMEM(tiled, F32), pltpu.VMEM((2, *tiled), F32),
        ]


def neighbours(win, count, lanes):
    mid = win[G : G + count]
    size = count + 2 * G
    up = pltpu.roll(win, 1, 0)[G : G + count]
    down = pltpu.roll(win, size - 1, 0)[G : G + count]
    before = pltpu.roll(mid, 1, 1)
    after = pltpu.roll(mid, lanes - 1, 1)
    return mid, up, down, before, after


def loop(start, count, step, body):
    for r in range(0, count, step):
        body(start + r, min(step, count - r))


def setup(level, k_ref, s_ref, a_ref, pairs=None, source=None):
    def body(r, count):
        mid, up, down, before, after = neighbours(
            k_ref[pl.ds(r, count + 2 * G), :], count, level.lanes
        )
        inside = mid > 0.0
        if not level.split:
            lane = iota(mid.shape, 1)
            before = jnp.where(lane == 0, 0.0, before)
            after = jnp.where(lane == level.lanes - 1, 0.0, after)
        west, east = 0.5 * (mid + up), 0.5 * (mid + down)
        south, north = 0.5 * (mid + before), 0.5 * (mid + after)
        rows = pl.ds(r, count)
        stored = s_ref[rows, :]
        diag = stored + west + east + south + north
        c = jnp.where(inside, OMEGA / diag, 0.0)
        a_ref[0, rows, :] = c * west
        a_ref[1, rows, :] = c * east
        if level.split:
            a_ref[2, rows, :] = c * south
            a_ref[3, rows, :] = c * north
        else:
            a_ref[2, rows, :] = jnp.where(lane == 0, 0.0, c * south)
            a_ref[3, rows, :] = jnp.where(lane == level.ny - 1, 0.0, c * north)
        a_ref[5, rows, :] = c
        a_ref[6, rows, :] = diag * (1.0 / OMEGA)
        if pairs is not None:
            put_tiles(pairs.at[0], rows, mid)
            put_tiles(pairs.at[1], rows, stored)
        if source is not None:
            a_ref[4, rows, :] = c * source[rows_of(r, count), :]

    loop(0, level.rows, level.step, body)


def rows_of(r, count):
    return pl.ds(r + G, count)


def smooth(level, src, a_ref, put, start=0, total=None):
    def body(r, count):
        mid, up, down, before, after = neighbours(
            src[pl.ds(r, count + 2 * G), :], count, level.lanes
        )
        rows = pl.ds(r, count)
        new = (1.0 - OMEGA) * mid + a_ref[4, rows, :]
        new = new + (a_ref[0, rows, :] * up + a_ref[1, rows, :] * down)
        new = new + (a_ref[2, rows, :] * before + a_ref[3, rows, :] * after)
        put(r, rows, mid, new)

    loop(start, level.rows if total is None else total, level.step, body)


def sweep(level, src, dst, a_ref, start=0, total=None):
    def put(r, rows, mid, new):
        dst[rows_of(r, rows.size), :] = new

    smooth(level, src, a_ref, put, start, total)


def residual(level, src, dst, a_ref):
    def put(r, rows, mid, new):
        put_tiles(dst, rows, (new - mid) * a_ref[6, rows, :])

    smooth(level, src, a_ref, put)


def residual_own(level, src, dst, a_ref):
    def put(r, rows, mid, new):
        part = (new - mid) * a_ref[6, rows, :]
        put_tiles(dst, pl.ds(r - level.halo, rows.size), part[:, : level.by])

    smooth(level, src, a_ref, put, level.halo, level.bx)


def lane_map(fine, coarse, lane):
    half = lane // 2
    if fine.split:
        shift = coarse.lanes - fine.lanes // 2
        half = jnp.where(lane >= fine.lanes - fine.halo, half + shift, half)
    return half


def matrices(fine, coarse, my):
    shape = (fine.by, coarse.by) if fine.depth == 0 else (fine.lanes, coarse.lanes)
    lane, there = iota(shape, 0), iota(shape, 1)
    if fine.depth == 0:
        down = lane // 2 == there
    elif fine.split and not coarse.split:
        down = (lane < fine.by) & (lane // 2 == there)
    else:
        down = lane_map(fine, coarse, lane) == there
    shape = (coarse.lanes, fine.lanes)
    there, lane = iota(shape, 0), iota(shape, 1)
    if fine.split and not coarse.split:
        col = jnp.where(lane >= fine.lanes - fine.halo, lane - fine.lanes, lane)
        gap = (lane >= fine.by + fine.halo) & (lane < fine.lanes - fine.halo)
        target = (col + my * fine.by + 2 * coarse.lanes) // 2 - coarse.lanes
        up = (there == target) & ~gap
    else:
        up = there == lane_map(fine, coarse, lane)
    return ones_where(down), ones_where(up)


def block_sum(x, count, factor, place):
    shape = (count, x.shape[0])
    rows = ones_where(iota(shape, 1) // factor == iota(shape, 0))
    shape = (x.shape[1], 128)
    cols = ones_where(iota(shape, 0) // factor + place == iota(shape, 1))
    return right(left(rows, x), cols)


class Exchange:
    def __init__(self, ext, scratch, level, here, size):
        self.ext, self.level = ext, level
        self.strips, self.halos = scratch[:2], scratch[2:4]
        self.mx, self.my = here
        self.dx, self.dy = size
        self.count, self.width = ext.shape[0], level.halo
        self.groups = 128 // (self.count * self.width)
        self.rows = level.bx // self.groups
        self.copies = []
        bx, by, w, rows = level.bx, level.by, self.width, self.rows
        for n, (sx, sy) in enumerate((i, j) for i in (-1, 0, 1) for j in (-1, 0, 1) if i or j):
            if sy == 0:
                first = G + w if sx < 0 else G + bx
                there = G + w + bx if sx < 0 else G
                src = ext.at[:, pl.ds(first, w), pl.ds(0, by)]
                dst = ext.at[:, pl.ds(there, w), pl.ds(0, by)]
            else:
                mine, theirs = (self.strips[0], self.halos[1]) if sy < 0 else (self.strips[1], self.halos[0])
                if sx == 0:
                    src, dst = mine, theirs.at[pl.ds(w, rows)]
                elif sx < 0:
                    src, dst = mine.at[pl.ds(0, w)], theirs.at[pl.ds(w + rows, w)]
                else:
                    src, dst = mine.at[pl.ds(rows - w, w)], theirs.at[pl.ds(0, w)]
            copy = pltpu.make_async_remote_copy(
                src_ref=src, dst_ref=dst, send_sem=scratch[4].at[n], recv_sem=scratch[5].at[n],
                device_id=(self.mx + sx, self.my + sy), device_id_type=MESH,
            )
            self.copies.append((copy, self.there(sx, sy), self.there(-sx, -sy)))

    @staticmethod
    def scratch(level, count):
        rows = level.bx * level.halo * count // 128
        strip, halo = pltpu.VMEM((rows, 128), F32), pltpu.VMEM((rows + 2 * level.halo, 128), F32)
        return [strip, strip, halo, halo, pltpu.SemaphoreType.DMA((8,)), pltpu.SemaphoreType.DMA((8,))]

    def there(self, sx, sy):
        x, y = self.mx + sx, self.my + sy
        return (x >= 0) & (x < self.dx) & (y >= 0) & (y < self.dy)

    def pack(self):
        level, w = self.level, self.width
        slot = iota((self.rows, 128), 1) // w
        for strip, first, at in ((self.strips[0], 0, 0), (self.strips[1], level.by - 128, 128 - w)):
            packed = None
            for i in range(self.count * self.groups):
                group, j = divmod(i, self.count)
                x = self.ext[j, pl.ds(G + w + group * self.rows, self.rows), pl.ds(first, 128)]
                turn = (w * i - at) % 128
                if turn:
                    x = pltpu.roll(x, turn, 1)
                packed = x if packed is None else jnp.where(slot == i, x, packed)
            strip[...] = packed

    def start(self):
        for copy, ok, _ in self.copies:
            pl.when(ok)(copy.start)

    def finish(self):
        for copy, _, back in self.copies:
            pl.when(back)(copy.wait_recv)
        level, w, rows = self.level, self.width, self.rows
        tile = pl.ds(level.lanes - 128, 128)
        blocks = [(0, w, self.groups - 1, G), (w + rows, w, 0, G + w + level.bx)]
        blocks += [(w, rows, g, G + w + g * rows) for g in range(self.groups)]
        for first, count, group, there in blocks:
            lower, upper = (ref[pl.ds(first, count), :] for ref in self.halos)
            lane = iota((count, 128), 1)
            right_part = (lane < w) & (self.my < self.dy - 1)
            left_part = (lane >= 128 - w) & (self.my > 0)
            for j in range(self.count):
                at = (group * self.count + j) * w
                turn_l, turn_r = (128 - w - at) % 128, -at % 128
                x = pltpu.roll(lower, turn_l, 1) if turn_l else lower
                y = pltpu.roll(upper, turn_r, 1) if turn_r else upper
                x = jnp.where(right_part, y, jnp.where(left_part, x, 0.0))
                self.ext[j, pl.ds(there, count), tile] = x
        for edge, first in ((self.mx == 0, G), (self.mx == self.dx - 1, G + w + level.bx)):
            @pl.when(edge)
            def _():
                self.ext[:, pl.ds(first, w), :] = jnp.zeros((self.count, w, level.lanes), F32)

    def drain(self):
        for copy, ok, _ in self.copies:
            pl.when(ok)(copy.wait_send)


def kernel(levels, dx, dy, *refs):
    p_hbm, s_hbm, k_hbm, st_hbm, out_ref = refs[:5]
    ext, ext_coef, ext_side, own_res, own_pairs, ga, gb, gca, gcb = refs[5:14]
    refs = refs[14:]
    ex_scratch, refs = [refs[:6], refs[6:12], refs[12:18]], refs[18:]
    held = []
    for _ in levels:
        held.append(list(refs[:7]))
        refs = refs[7:]
    downs, ups = refs[: LEVELS - 1], refs[LEVELS - 1 : 2 * LEVELS - 2]
    refs = refs[2 * LEVELS - 2 :]
    stage, out_sem, load_sem, y_send, y_recv, x_send, x_recv = refs

    mx, my = lax.axis_index("gx"), lax.axis_index("gy")
    top, second = levels[:2]
    bx, by = top.bx, top.by
    own = pl.ds(G + top.halo, bx)
    held[1][3], held[1][4] = ext_coef.at[0], ext_coef.at[1, pl.ds(G, second.rows)]

    loads, tiled_loads = [], []
    for i, ref in enumerate((p_hbm, s_hbm, k_hbm, st_hbm)):
        loads.append(pltpu.make_async_copy(ref, ext.at[i, own, pl.ds(0, by)], load_sem.at[i]))
        loads[-1].start()
    for i, ref in enumerate((k_hbm, st_hbm)):
        for t in range(by // 128):
            tiled_loads.append(pltpu.make_async_copy(
                ref.at[:, pl.ds(128 * t, 128)], own_pairs.at[i, t], load_sem.at[4 + i * (by // 128) + t]
            ))
            tiled_loads[-1].start()

    halo = Exchange(ext, ex_scratch[0], top, (mx, my), (dx, dy))
    halo_coef = Exchange(ext_coef, ex_scratch[1], second, (mx, my), (dx, dy))
    halo_side = Exchange(ext_side, ex_scratch[2], second, (mx, my), (dx, dy))

    barrier = pltpu.get_barrier_semaphore()
    for d in range(1, dx):
        pl.semaphore_signal(barrier, inc=1, device_id=(lax.rem(mx + d, dx), my), device_id_type=MESH)
    for d in range(1, dy):
        pl.semaphore_signal(barrier, inc=1, device_id=(mx, lax.rem(my + d, dy)), device_id_type=MESH)
    signals = dx - 1 + dy - 1
    for sx in (-1, 1):
        for sy in (-1, 1):
            ok = halo.there(sx, sy)
            signals = signals + jnp.where(ok, 1, 0)
            @pl.when(ok)
            def _():
                pl.semaphore_signal(barrier, inc=1, device_id=(mx + sx, my + sy), device_id_type=MESH)

    for ref, level in ((ext.at[0], top), (ext.at[2], top), (ext_coef.at[0], second)):
        ref[0:G, :] = jnp.zeros((G, level.lanes), F32)
        ref[G + level.rows :, :] = jnp.zeros((G, level.lanes), F32)
    for level, (a, v, u, k, s, r, c) in zip(levels, held):
        for ref in (v, u, k):
            ref[0:G, :] = jnp.zeros((G, level.lanes), F32)
            ref[G + level.rows :, :] = jnp.zeros((G, level.lanes), F32)
    downs[0][...] = matrices(top, second, my)[0]

    for copy in loads:
        copy.wait()
    halo.pack()
    pl.semaphore_wait(barrier, signals)
    halo.start()

    for copy in tiled_loads:
        copy.wait()
    half = bx // 2
    own_second = pl.ds(G + second.halo, half)
    both = jnp.concatenate([pair_rows(own_pairs.at[0]), pair_rows(own_pairs.at[1])], axis=0)
    both = right(both, downs[0][...])
    near_k, near_s = 0.5 * both[:half], both[half:]
    ext_coef[0, own_second, 0 : by // 2] = near_k
    ext_coef[1, own_second, 0 : by // 2] = near_s

    whole = levels[LOCAL]
    factor = 1 << LOCAL
    gx_rows, gy_cols = bx // factor, by // factor
    sends = []

    def send(src, dst, sems, n, target):
        copy = pltpu.make_async_remote_copy(
            src_ref=src, dst_ref=dst, send_sem=sems[0].at[n], recv_sem=sems[1].at[n],
            device_id=target, device_id_type=MESH,
        )
        copy.start()
        sends.append(copy)
        return copy

    def over_gy(buffer, base):
        return [
            send(buffer.at[my], buffer.at[my], (y_send, y_recv), base + d, (mx, lax.rem(my + d, dy)))
            for d in range(1, dy)
        ]

    def strip_of(row):
        return pl.ds(pl.multiple_of(row * gx_rows, 8), gx_rows)

    far_k = 0.5 ** (LOCAL - 1) * block_sum(near_k, gx_rows, factor // 2, 0)
    gca[my] = far_k + block_sum(near_s, gx_rows, factor // 2, gy_cols)
    coef_y = over_gy(gca, 0)
    halo_coef.pack()
    halo_coef.start()

    for depth in range(1, LOCAL):
        downs[depth][...] = matrices(levels[depth], levels[depth + 1], my)[0]

    halo.finish()
    setup(top, ext.at[2], ext.at[3, pl.ds(G, top.rows)], held[0][0], None, ext.at[1])

    for copy in coef_y:
        copy.wait_recv()

    def merge(ref, i):
        shape = (ref.shape[1], whole.lanes)
        lane = iota(shape, 1)
        merged = jnp.zeros(shape, F32)
        for j in range(dy):
            first = gy_cols * j
            x = jnp.concatenate([ref[j]] * (whole.lanes // 128), axis=1)
            turn = (first - gy_cols * i) % whole.lanes
            x = pltpu.roll(x, turn, 1) if turn else x
            merged = jnp.where((lane >= first) & (lane < first + gy_cols), x, merged)
        return merged

    for i in range(2):
        gcb[i, strip_of(mx), :] = merge(gca, i)
    mine = gcb.at[:, strip_of(mx)]
    coef_x = [
        send(mine, mine, (x_send, x_recv), d, (lax.rem(mx + d, dx), my)) for d in range(2, dx, 2)
    ]

    def coarse_terms(depth):
        level = levels[depth]
        a, _, _, k, s, _, pairs = held[depth]
        fine = held[depth - 1][6]
        both = jnp.concatenate([pair_rows(fine.at[0]), pair_rows(fine.at[1])], axis=0)
        both = right(both, downs[depth - 1][...])
        k[pl.ds(G, level.rows), :] = 0.5 * both[: level.rows]
        s[...] = both[level.rows :]
        needed = depth != LOCAL - 1 and depth != LEVELS - 1
        setup(level, k, s, a, pairs if needed else None)

    def first_sweep(depth, side):
        level = levels[depth]
        a, v = held[depth][:2]
        first = a[5] * side
        a[4] = first
        v[pl.ds(G, level.rows), :] = first

    sweep(top, ext.at[0], held[0][1], held[0][0])
    sweep(top, held[0][1], held[0][2], held[0][0])
    residual_own(top, held[0][2], own_res, held[0][0])
    ext_side[0, own_second, 0 : by // 2] = right(pair_rows(own_res), downs[0][...])
    halo_side.pack()
    halo_side.start()

    halo_coef.finish()
    setup(second, held[1][3], held[1][4], held[1][0], held[1][6])
    for depth in range(2, LOCAL):
        coarse_terms(depth)
    for copy in coef_x:
        copy.wait_recv()
    core = lax.rem(mx, 2)
    coef_x = []
    for chip in range(dx // 2):
        part = gcb.at[:, strip_of(2 * chip + core)]
        coef_x.append(send(part, part, (x_send, x_recv), 2 * dx + chip, (mx + 1 - 2 * core, my)))

    halo_side.finish()
    for depth in range(1, LOCAL):
        level = levels[depth]
        a, v, u, k, s, res, _ = held[depth]
        if depth == 1:
            first_sweep(depth, ext_side[0, pl.ds(G, level.rows), :])
        else:
            first_sweep(depth, right(pair_rows(held[depth - 1][5]), downs[depth - 1][...]))
        sweep(level, v, u, a)
        residual(level, u, res, a)

    last = levels[LOCAL - 1]
    edge = last.halo // 2
    side = right(pair_rows(held[LOCAL - 1][5]), downs[LOCAL - 1][...])
    packed = 128 // gy_cols
    count = gx_rows // packed
    strip = side[edge : edge + count, :128]
    for g in range(1, packed):
        strip = strip + pltpu.roll(side[edge + g * count : edge + (g + 1) * count, :128], g * gy_cols, 1)
    ga[my] = strip
    side_y = over_gy(ga, dy)

    for copy in coef_x:
        copy.wait_recv()
    a, _, _, k, s, _, pairs = held[LOCAL]
    k[pl.ds(G, whole.rows), :] = gcb[0]
    s[...] = gcb[1]
    setup(whole, k, s, a, pairs)

    for copy in side_y:
        copy.wait_recv()
    for g in range(packed):
        gb[pl.ds(pl.multiple_of(mx * gx_rows + g * count, 8), count), :] = merge(ga, g)
    mine = gb.at[strip_of(mx)]
    side_x = [
        send(mine, mine, (x_send, x_recv), dx + d, (lax.rem(mx + d, dx), my)) for d in range(1, dx)
    ]

    for depth in range(LEVELS - 1):
        down, ups[depth][...] = matrices(levels[depth], levels[depth + 1], my)
        if depth >= LOCAL:
            downs[depth][...] = down
    for depth in range(LOCAL + 1, LEVELS):
        coarse_terms(depth)

    for copy in side_x:
        copy.wait_recv()

    for depth in range(LOCAL, LEVELS):
        level = levels[depth]
        a, v, u, k, s, res, _ = held[depth]
        if depth == LOCAL:
            first_sweep(depth, gb[...])
        else:
            first_sweep(depth, right(pair_rows(held[depth - 1][5]), downs[depth - 1][...]))
        if depth < LEVELS - 1:
            sweep(level, v, u, a)
            residual(level, u, res, a)
        else:
            for i in range(COARSE_SWEEPS - 1):
                sweep(level, *((v, u) if i % 2 == 0 else (u, v)), a)
            if COARSE_SWEEPS % 2:
                u[...] = v[...]

    for depth in reversed(range(LEVELS - 1)):
        level, below = levels[depth], levels[depth + 1]
        a, v, u, k, s, res, _ = held[depth]
        error = held[depth + 1][2]
        if depth == LOCAL - 1:
            window = error[pl.ds(pl.multiple_of(mx * gx_rows, 8), gx_rows + 2 * G), :]
            wide = right(window, ups[depth][...])[G - edge : G + gx_rows + edge]
        else:
            skip = below.halo - level.halo // 2
            wide = right(error[pl.ds(G + skip, below.rows - 2 * skip), :], ups[depth][...])
        repeat_rows(res, wide)
        tiles = [res[t] for t in range(level.lanes // 128)]
        u[pl.ds(G, level.rows), :] += jnp.concatenate(tiles, axis=1)
        if depth:
            sweep(level, u, v, a)
            sweep(level, v, u, a)
        else:
            sweep(level, u, v, a)

            def put(r, rows, mid, new):
                stage[pl.ds(r - level.halo, rows.size), :] = (1.0 / OMEGA) * new[:, :by]

            half = bx // 2
            results = []
            for i in range(2):
                smooth(level, v, a, put, level.halo + i * half, half)
                part = pl.ds(i * half, half)
                results.append(pltpu.make_async_copy(stage.at[part], out_ref.at[part], out_sem.at[i]))
                results[-1].start()

    for exchange in (halo, halo_coef, halo_side):
        exchange.drain()
    for copy in sends:
        copy.wait_send()
    for copy in results:
        copy.wait()


def per_device(nx, ny, pressure, source, conductivity, storage):
    dx, dy = lax.axis_size("gx"), lax.axis_size("gy")
    bx, by = pressure.shape
    levels = [Level(depth, bx, by, nx, ny) for depth in range(LEVELS)]
    top, second, whole = levels[0], levels[1], levels[LOCAL]
    rows, tiles = bx >> LOCAL, by // 128
    scratch = [
        pltpu.VMEM((4, top.rows + 2 * G, top.lanes), F32),
        pltpu.VMEM((2, second.rows + 2 * G, second.lanes), F32),
        pltpu.VMEM((1, second.rows + 2 * G, second.lanes), F32),
        pltpu.VMEM((tiles, bx, 128), F32),
        pltpu.VMEM((2, tiles, bx, 128), F32),
        pltpu.VMEM((dy, rows * (by >> LOCAL) // 128, 128), F32),
        pltpu.VMEM((whole.rows, whole.lanes), F32),
        pltpu.VMEM((dy, rows, 128), F32),
        pltpu.VMEM((2, whole.rows, whole.lanes), F32),
    ]
    for level, count in ((top, 4), (second, 2), (second, 1)):
        scratch += Exchange.scratch(level, count)
    for level in levels:
        scratch += level.scratch()
    pairs = list(zip(levels, levels[1:]))
    scratch += [
        pltpu.VMEM((fine.lanes, coarse.lanes) if fine.depth else (by, by // 2), jnp.bfloat16)
        for fine, coarse in pairs
    ]
    scratch += [pltpu.VMEM((coarse.lanes, fine.lanes), jnp.bfloat16) for fine, coarse in pairs]
    scratch += [
        pltpu.VMEM((bx, by), F32),
        pltpu.SemaphoreType.DMA((2,)),
        pltpu.SemaphoreType.DMA((4 + 2 * tiles,)),
        pltpu.SemaphoreType.DMA((2 * dy,)),
        pltpu.SemaphoreType.DMA((2 * dy,)),
        pltpu.SemaphoreType.DMA((3 * dx,)),
        pltpu.SemaphoreType.DMA((3 * dx,)),
    ]
    result = pl.pallas_call(
        functools.partial(kernel, levels, dx, dy),
        out_shape=jax.ShapeDtypeStruct((bx, by), F32),
        in_specs=[pl.BlockSpec(memory_space=pltpu.HBM)] * 4,
        out_specs=pl.BlockSpec(memory_space=pltpu.HBM),
        scratch_shapes=scratch,
        compiler_params=pltpu.CompilerParams(
            collective_id=0, has_side_effects=True, vmem_limit_bytes=62 * 2**20
        ),
    )(pressure, source, conductivity, storage)
    return OMEGA * result


def solution(mesh):
    placed = (P("gx", "gy"), P("gx", "gy"), P("gx", "gy"), P("gx", "gy"))

    def run(pressure, source, conductivity, storage):
        nx, ny = pressure.shape
        return jax.shard_map(
            functools.partial(per_device, nx, ny),
            mesh=mesh, in_specs=placed, out_specs=P("gx", "gy"), check_vma=False,
        )(pressure, source, conductivity, storage)

    return run
```

```python
import functools

import jax
import jax.numpy as jnp
from jax import lax
from jax.experimental import pallas as pl
from jax.experimental.pallas import tpu as pltpu
from jax.sharding import PartitionSpec as P

LEVELS_SPLIT = 4
LEVELS_MERGED = 2
COARSE_SWEEPS = 8
OMEGA = 0.8

LOCAL = LEVELS_SPLIT - 1
LEVELS = LEVELS_SPLIT + LEVELS_MERGED
HALOS = (8, 16, 8)
G = 8
MESH = pl.DeviceIdType.MESH
F32 = jnp.float32


def round_up(n, m):
    return -(-n // m) * m


def iota(shape, dim):
    return lax.broadcasted_iota(jnp.int32, shape, dim)


def ones_where(mask):
    return jnp.where(mask, 1.0, 0.0).astype(jnp.bfloat16)


def parts(x):
    high = x.astype(jnp.bfloat16)
    low = (x - high.astype(F32)).astype(jnp.bfloat16)
    return high, low


def dot(a, b):
    return jnp.dot(a, b, preferred_element_type=F32)


def left(matrix, x):
    high, low = parts(x)
    return dot(matrix, high) + dot(matrix, low)


def right(x, matrix):
    high, low = parts(x)
    return dot(high, matrix) + dot(low, matrix)


def put_tiles(ref, rows, x):
    for t in range(x.shape[1] // 128):
        ref[t, rows, :] = x[:, 128 * t : 128 * t + 128]


def pair_rows(ref):
    tiles, rows, _ = ref.shape
    first, second = pl.ds(0, rows // 2, stride=2), pl.ds(1, rows // 2, stride=2)
    return jnp.concatenate([ref[t, first, :] + ref[t, second, :] for t in range(tiles)], axis=1)


def repeat_rows(ref, x):
    tiles, rows, _ = ref.shape
    for t in range(tiles):
        part = x[:, 128 * t : 128 * t + 128]
        ref[t, pl.ds(0, rows // 2, stride=2), :] = part
        ref[t, pl.ds(1, rows // 2, stride=2), :] = part


class Level:
    def __init__(self, depth, bx, by, nx, ny):
        self.depth = depth
        self.split = depth < LOCAL
        self.nx, self.ny = nx >> depth, ny >> depth
        if self.split:
            self.halo = HALOS[depth]
            self.bx, self.by = bx >> depth, by >> depth
            self.rows = self.bx + 2 * self.halo
            self.lanes = round_up(self.by + 2 * self.halo, 128)
        else:
            self.halo = 0
            self.bx, self.by = self.nx, self.ny
            self.rows = self.nx
            self.lanes = round_up(self.ny, 128)
        self.step = 32 if self.lanes > 128 else 128

    def scratch(self):
        tall = pltpu.VMEM((self.rows + 2 * G, self.lanes), F32)
        flat = pltpu.VMEM((self.rows, self.lanes), F32)
        tiled = (self.lanes // 128, self.rows, 128)
        return [
            pltpu.VMEM((7, self.rows, self.lanes), F32), tall, tall, tall, flat,
            pltpu.VMEM(tiled, F32), pltpu.VMEM((2, *tiled), F32),
        ]


def neighbours(win, count, lanes):
    mid = win[G : G + count]
    size = count + 2 * G
    up = pltpu.roll(win, 1, 0)[G : G + count]
    down = pltpu.roll(win, size - 1, 0)[G : G + count]
    before = pltpu.roll(mid, 1, 1)
    after = pltpu.roll(mid, lanes - 1, 1)
    return mid, up, down, before, after


def loop(start, count, step, body):
    for r in range(0, count, step):
        body(start + r, min(step, count - r))


def setup(level, k_ref, s_ref, a_ref, pairs=None, source=None):
    def body(r, count):
        mid, up, down, before, after = neighbours(
            k_ref[pl.ds(r, count + 2 * G), :], count, level.lanes
        )
        inside = mid > 0.0
        if not level.split:
            lane = iota(mid.shape, 1)
            before = jnp.where(lane == 0, 0.0, before)
            after = jnp.where(lane == level.lanes - 1, 0.0, after)
        west, east = 0.5 * (mid + up), 0.5 * (mid + down)
        south, north = 0.5 * (mid + before), 0.5 * (mid + after)
        rows = pl.ds(r, count)
        stored = s_ref[rows, :]
        diag = stored + west + east + south + north
        c = jnp.where(inside, OMEGA / diag, 0.0)
        a_ref[0, rows, :] = c * west
        a_ref[1, rows, :] = c * east
        if level.split:
            a_ref[2, rows, :] = c * south
            a_ref[3, rows, :] = c * north
        else:
            a_ref[2, rows, :] = jnp.where(lane == 0, 0.0, c * south)
            a_ref[3, rows, :] = jnp.where(lane == level.ny - 1, 0.0, c * north)
        a_ref[5, rows, :] = c
        a_ref[6, rows, :] = diag * (1.0 / OMEGA)
        if pairs is not None:
            put_tiles(pairs.at[0], rows, mid)
            put_tiles(pairs.at[1], rows, stored)
        if source is not None:
            a_ref[4, rows, :] = c * source[rows_of(r, count), :]

    loop(0, level.rows, level.step, body)


def rows_of(r, count):
    return pl.ds(r + G, count)


def smooth(level, src, a_ref, put, start=0, total=None):
    def body(r, count):
        mid, up, down, before, after = neighbours(
            src[pl.ds(r, count + 2 * G), :], count, level.lanes
        )
        rows = pl.ds(r, count)
        new = (1.0 - OMEGA) * mid + a_ref[4, rows, :]
        new = new + (a_ref[0, rows, :] * up + a_ref[1, rows, :] * down)
        new = new + (a_ref[2, rows, :] * before + a_ref[3, rows, :] * after)
        put(r, rows, mid, new)

    loop(start, level.rows if total is None else total, level.step, body)


def sweep(level, src, dst, a_ref, start=0, total=None):
    def put(r, rows, mid, new):
        dst[rows_of(r, rows.size), :] = new

    smooth(level, src, a_ref, put, start, total)


def residual(level, src, dst, a_ref):
    def put(r, rows, mid, new):
        put_tiles(dst, rows, (new - mid) * a_ref[6, rows, :])

    smooth(level, src, a_ref, put)


def residual_own(level, src, dst, a_ref):
    def put(r, rows, mid, new):
        part = (new - mid) * a_ref[6, rows, :]
        put_tiles(dst, pl.ds(r - level.halo, rows.size), part[:, : level.by])

    smooth(level, src, a_ref, put, level.halo, level.bx)


def lane_map(fine, coarse, lane):
    half = lane // 2
    if fine.split:
        shift = coarse.lanes - fine.lanes // 2
        half = jnp.where(lane >= fine.lanes - fine.halo, half + shift, half)
    return half


def matrices(fine, coarse, my):
    shape = (fine.by, coarse.by) if fine.depth == 0 else (fine.lanes, coarse.lanes)
    lane, there = iota(shape, 0), iota(shape, 1)
    if fine.depth == 0:
        down = lane // 2 == there
    elif fine.split and not coarse.split:
        down = (lane < fine.by) & (lane // 2 == there)
    else:
        down = lane_map(fine, coarse, lane) == there
    shape = (coarse.lanes, fine.lanes)
    there, lane = iota(shape, 0), iota(shape, 1)
    if fine.split and not coarse.split:
        col = jnp.where(lane >= fine.lanes - fine.halo, lane - fine.lanes, lane)
        gap = (lane >= fine.by + fine.halo) & (lane < fine.lanes - fine.halo)
        target = (col + my * fine.by + 2 * coarse.lanes) // 2 - coarse.lanes
        up = (there == target) & ~gap
    else:
        up = there == lane_map(fine, coarse, lane)
    return ones_where(down), ones_where(up)


def block_sum(x, count, factor, place):
    shape = (count, x.shape[0])
    rows = ones_where(iota(shape, 1) // factor == iota(shape, 0))
    shape = (x.shape[1], 128)
    cols = ones_where(iota(shape, 0) // factor + place == iota(shape, 1))
    return right(left(rows, x), cols)


class Exchange:
    def __init__(self, ext, scratch, level, here, size):
        self.ext, self.level = ext, level
        self.strips, self.halos = scratch[:2], scratch[2:4]
        self.mx, self.my = here
        self.dx, self.dy = size
        self.count, self.width = ext.shape[0], level.halo
        self.groups = 128 // (self.count * self.width)
        self.rows = level.bx // self.groups
        self.copies = []
        bx, by, w, rows = level.bx, level.by, self.width, self.rows
        for n, (sx, sy) in enumerate((i, j) for i in (-1, 0, 1) for j in (-1, 0, 1) if i or j):
            if sy == 0:
                first = G + w if sx < 0 else G + bx
                there = G + w + bx if sx < 0 else G
                src = ext.at[:, pl.ds(first, w), pl.ds(0, by)]
                dst = ext.at[:, pl.ds(there, w), pl.ds(0, by)]
            else:
                mine, theirs = (self.strips[0], self.halos[1]) if sy < 0 else (self.strips[1], self.halos[0])
                if sx == 0:
                    src, dst = mine, theirs.at[pl.ds(w, rows)]
                elif sx < 0:
                    src, dst = mine.at[pl.ds(0, w)], theirs.at[pl.ds(w + rows, w)]
                else:
                    src, dst = mine.at[pl.ds(rows - w, w)], theirs.at[pl.ds(0, w)]
            copy = pltpu.make_async_remote_copy(
                src_ref=src, dst_ref=dst, send_sem=scratch[4].at[n], recv_sem=scratch[5].at[n],
                device_id=(self.mx + sx, self.my + sy), device_id_type=MESH,
            )
            self.copies.append((copy, self.there(sx, sy), self.there(-sx, -sy)))

    @staticmethod
    def scratch(level, count):
        rows = level.bx * level.halo * count // 128
        strip, halo = pltpu.VMEM((rows, 128), F32), pltpu.VMEM((rows + 2 * level.halo, 128), F32)
        return [strip, strip, halo, halo, pltpu.SemaphoreType.DMA((8,)), pltpu.SemaphoreType.DMA((8,))]

    def there(self, sx, sy):
        x, y = self.mx + sx, self.my + sy
        return (x >= 0) & (x < self.dx) & (y >= 0) & (y < self.dy)

    def pack(self):
        level, w = self.level, self.width
        slot = iota((self.rows, 128), 1) // w
        for strip, first, at in ((self.strips[0], 0, 0), (self.strips[1], level.by - 128, 128 - w)):
            packed = None
            for i in range(self.count * self.groups):
                group, j = divmod(i, self.count)
                x = self.ext[j, pl.ds(G + w + group * self.rows, self.rows), pl.ds(first, 128)]
                turn = (w * i - at) % 128
                if turn:
                    x = pltpu.roll(x, turn, 1)
                packed = x if packed is None else jnp.where(slot == i, x, packed)
            strip[...] = packed

    def start(self):
        for copy, ok, _ in self.copies:
            pl.when(ok)(copy.start)

    def finish(self):
        for copy, _, back in self.copies:
            pl.when(back)(copy.wait_recv)
        level, w, rows = self.level, self.width, self.rows
        tile = pl.ds(level.lanes - 128, 128)
        blocks = [(0, w, self.groups - 1, G), (w + rows, w, 0, G + w + level.bx)]
        blocks += [(w, rows, g, G + w + g * rows) for g in range(self.groups)]
        for first, count, group, there in blocks:
            lower, upper = (ref[pl.ds(first, count), :] for ref in self.halos)
            lane = iota((count, 128), 1)
            right_part = (lane < w) & (self.my < self.dy - 1)
            left_part = (lane >= 128 - w) & (self.my > 0)
            for j in range(self.count):
                at = (group * self.count + j) * w
                turn_l, turn_r = (128 - w - at) % 128, -at % 128
                x = pltpu.roll(lower, turn_l, 1) if turn_l else lower
                y = pltpu.roll(upper, turn_r, 1) if turn_r else upper
                x = jnp.where(right_part, y, jnp.where(left_part, x, 0.0))
                self.ext[j, pl.ds(there, count), tile] = x
        for edge, first in ((self.mx == 0, G), (self.mx == self.dx - 1, G + w + level.bx)):
            @pl.when(edge)
            def _():
                self.ext[:, pl.ds(first, w), :] = jnp.zeros((self.count, w, level.lanes), F32)

    def drain(self):
        for copy, ok, _ in self.copies:
            pl.when(ok)(copy.wait_send)


def kernel(levels, dx, dy, *refs):
    p_hbm, s_hbm, k_hbm, st_hbm, out_ref = refs[:5]
    ext, ext_coef, ext_side, own_res, own_pairs, ga, gb, gca, gcb = refs[5:14]
    refs = refs[14:]
    ex_scratch, refs = [refs[:6], refs[6:12], refs[12:18]], refs[18:]
    held = []
    for _ in levels:
        held.append(list(refs[:7]))
        refs = refs[7:]
    downs, ups = refs[: LEVELS - 1], refs[LEVELS - 1 : 2 * LEVELS - 2]
    refs = refs[2 * LEVELS - 2 :]
    load_sem, y_send, y_recv, x_send, x_recv = refs

    mx, my = lax.axis_index("gx"), lax.axis_index("gy")
    top, second = levels[:2]
    bx, by = top.bx, top.by
    own = pl.ds(G + top.halo, bx)
    held[1][3], held[1][4] = ext_coef.at[0], ext_coef.at[1, pl.ds(G, second.rows)]

    loads, tiled_loads = [], []
    for i, ref in enumerate((p_hbm, s_hbm, k_hbm, st_hbm)):
        loads.append(pltpu.make_async_copy(ref, ext.at[i, own, pl.ds(0, by)], load_sem.at[i]))
        loads[-1].start()
    for i, ref in enumerate((k_hbm, st_hbm)):
        for t in range(by // 128):
            tiled_loads.append(pltpu.make_async_copy(
                ref.at[:, pl.ds(128 * t, 128)], own_pairs.at[i, t], load_sem.at[4 + i * (by // 128) + t]
            ))
            tiled_loads[-1].start()

    halo = Exchange(ext, ex_scratch[0], top, (mx, my), (dx, dy))
    halo_coef = Exchange(ext_coef, ex_scratch[1], second, (mx, my), (dx, dy))
    halo_side = Exchange(ext_side, ex_scratch[2], second, (mx, my), (dx, dy))

    barrier = pltpu.get_barrier_semaphore()
    for d in range(1, dx):
        pl.semaphore_signal(barrier, inc=1, device_id=(lax.rem(mx + d, dx), my), device_id_type=MESH)
    for d in range(1, dy):
        pl.semaphore_signal(barrier, inc=1, device_id=(mx, lax.rem(my + d, dy)), device_id_type=MESH)
    signals = dx - 1 + dy - 1
    for sx in (-1, 1):
        for sy in (-1, 1):
            ok = halo.there(sx, sy)
            signals = signals + jnp.where(ok, 1, 0)
            @pl.when(ok)
            def _():
                pl.semaphore_signal(barrier, inc=1, device_id=(mx + sx, my + sy), device_id_type=MESH)

    for ref, level in ((ext.at[0], top), (ext.at[2], top), (ext_coef.at[0], second)):
        ref[0:G, :] = jnp.zeros((G, level.lanes), F32)
        ref[G + level.rows :, :] = jnp.zeros((G, level.lanes), F32)
    for level, (a, v, u, k, s, r, c) in zip(levels, held):
        for ref in (v, u, k):
            ref[0:G, :] = jnp.zeros((G, level.lanes), F32)
            ref[G + level.rows :, :] = jnp.zeros((G, level.lanes), F32)
    downs[0][...] = matrices(top, second, my)[0]

    for copy in loads:
        copy.wait()
    halo.pack()
    pl.semaphore_wait(barrier, signals)
    halo.start()

    for copy in tiled_loads:
        copy.wait()
    half = bx // 2
    own_second = pl.ds(G + second.halo, half)
    both = jnp.concatenate([pair_rows(own_pairs.at[0]), pair_rows(own_pairs.at[1])], axis=0)
    both = right(both, downs[0][...])
    near_k, near_s = 0.5 * both[:half], both[half:]
    ext_coef[0, own_second, 0 : by // 2] = near_k
    ext_coef[1, own_second, 0 : by // 2] = near_s

    whole = levels[LOCAL]
    factor = 1 << LOCAL
    gx_rows, gy_cols = bx // factor, by // factor
    sends = []

    def send(src, dst, sems, n, target):
        copy = pltpu.make_async_remote_copy(
            src_ref=src, dst_ref=dst, send_sem=sems[0].at[n], recv_sem=sems[1].at[n],
            device_id=target, device_id_type=MESH,
        )
        copy.start()
        sends.append(copy)
        return copy

    def over_gy(buffer, base):
        return [
            send(buffer.at[my], buffer.at[my], (y_send, y_recv), base + d, (mx, lax.rem(my + d, dy)))
            for d in range(1, dy)
        ]

    def strip_of(row):
        return pl.ds(pl.multiple_of(row * gx_rows, 8), gx_rows)

    far_k = 0.5 ** (LOCAL - 1) * block_sum(near_k, gx_rows, factor // 2, 0)
    gca[my] = far_k + block_sum(near_s, gx_rows, factor // 2, gy_cols)
    coef_y = over_gy(gca, 0)
    halo_coef.pack()
    halo_coef.start()

    for depth in range(1, LOCAL):
        downs[depth][...] = matrices(levels[depth], levels[depth + 1], my)[0]

    halo.finish()
    setup(top, ext.at[2], ext.at[3, pl.ds(G, top.rows)], held[0][0], None, ext.at[1])

    for copy in coef_y:
        copy.wait_recv()

    def merge(ref, i):
        shape = (ref.shape[1], whole.lanes)
        lane = iota(shape, 1)
        merged = jnp.zeros(shape, F32)
        for j in range(dy):
            first = gy_cols * j
            x = jnp.concatenate([ref[j]] * (whole.lanes // 128), axis=1)
            turn = (first - gy_cols * i) % whole.lanes
            x = pltpu.roll(x, turn, 1) if turn else x
            merged = jnp.where((lane >= first) & (lane < first + gy_cols), x, merged)
        return merged

    for i in range(2):
        gcb[i, strip_of(mx), :] = merge(gca, i)
    mine = gcb.at[:, strip_of(mx)]
    coef_x = [
        send(mine, mine, (x_send, x_recv), d, (lax.rem(mx + d, dx), my)) for d in range(2, dx, 2)
    ]

    def coarse_terms(depth):
        level = levels[depth]
        a, _, _, k, s, _, pairs = held[depth]
        fine = held[depth - 1][6]
        both = jnp.concatenate([pair_rows(fine.at[0]), pair_rows(fine.at[1])], axis=0)
        both = right(both, downs[depth - 1][...])
        k[pl.ds(G, level.rows), :] = 0.5 * both[: level.rows]
        s[...] = both[level.rows :]
        needed = depth != LOCAL - 1 and depth != LEVELS - 1
        setup(level, k, s, a, pairs if needed else None)

    def first_sweep(depth, side):
        level = levels[depth]
        a, v = held[depth][:2]
        first = a[5] * side
        a[4] = first
        v[pl.ds(G, level.rows), :] = first

    sweep(top, ext.at[0], held[0][1], held[0][0])
    sweep(top, held[0][1], held[0][2], held[0][0])
    residual_own(top, held[0][2], own_res, held[0][0])
    ext_side[0, own_second, 0 : by // 2] = right(pair_rows(own_res), downs[0][...])
    halo_side.pack()
    halo_side.start()

    halo_coef.finish()
    setup(second, held[1][3], held[1][4], held[1][0], held[1][6])
    for depth in range(2, LOCAL):
        coarse_terms(depth)
    for copy in coef_x:
        copy.wait_recv()
    core = lax.rem(mx, 2)
    coef_x = []
    for chip in range(dx // 2):
        part = gcb.at[:, strip_of(2 * chip + core)]
        coef_x.append(send(part, part, (x_send, x_recv), 2 * dx + chip, (mx + 1 - 2 * core, my)))

    halo_side.finish()
    for depth in range(1, LOCAL):
        level = levels[depth]
        a, v, u, k, s, res, _ = held[depth]
        if depth == 1:
            first_sweep(depth, ext_side[0, pl.ds(G, level.rows), :])
        else:
            first_sweep(depth, right(pair_rows(held[depth - 1][5]), downs[depth - 1][...]))
        sweep(level, v, u, a)
        residual(level, u, res, a)

    last = levels[LOCAL - 1]
    edge = last.halo // 2
    side = right(pair_rows(held[LOCAL - 1][5]), downs[LOCAL - 1][...])
    packed = 128 // gy_cols
    count = gx_rows // packed
    strip = side[edge : edge + count, :128]
    for g in range(1, packed):
        strip = strip + pltpu.roll(side[edge + g * count : edge + (g + 1) * count, :128], g * gy_cols, 1)
    ga[my] = strip
    side_y = over_gy(ga, dy)

    for copy in coef_x:
        copy.wait_recv()
    a, _, _, k, s, _, pairs = held[LOCAL]
    k[pl.ds(G, whole.rows), :] = gcb[0]
    s[...] = gcb[1]
    setup(whole, k, s, a, pairs)

    for copy in side_y:
        copy.wait_recv()
    for g in range(packed):
        gb[pl.ds(pl.multiple_of(mx * gx_rows + g * count, 8), count), :] = merge(ga, g)
    mine = gb.at[strip_of(mx)]
    side_x = [
        send(mine, mine, (x_send, x_recv), dx + d, (lax.rem(mx + d, dx), my)) for d in range(1, dx)
    ]

    for depth in range(LEVELS - 1):
        down, ups[depth][...] = matrices(levels[depth], levels[depth + 1], my)
        if depth >= LOCAL:
            downs[depth][...] = down
    for depth in range(LOCAL + 1, LEVELS):
        coarse_terms(depth)

    for copy in side_x:
        copy.wait_recv()

    for depth in range(LOCAL, LEVELS):
        level = levels[depth]
        a, v, u, k, s, res, _ = held[depth]
        if depth == LOCAL:
            first_sweep(depth, gb[...])
        else:
            first_sweep(depth, right(pair_rows(held[depth - 1][5]), downs[depth - 1][...]))
        if depth < LEVELS - 1:
            sweep(level, v, u, a)
            residual(level, u, res, a)
        else:
            for i in range(COARSE_SWEEPS - 1):
                sweep(level, *((v, u) if i % 2 == 0 else (u, v)), a)
            if COARSE_SWEEPS % 2:
                u[...] = v[...]

    for depth in reversed(range(LEVELS - 1)):
        level, below = levels[depth], levels[depth + 1]
        a, v, u, k, s, res, _ = held[depth]
        error = held[depth + 1][2]
        if depth == LOCAL - 1:
            window = error[pl.ds(pl.multiple_of(mx * gx_rows, 8), gx_rows + 2 * G), :]
            wide = right(window, ups[depth][...])[G - edge : G + gx_rows + edge]
        else:
            skip = below.halo - level.halo // 2
            wide = right(error[pl.ds(G + skip, below.rows - 2 * skip), :], ups[depth][...])
        repeat_rows(res, wide)
        tiles = [res[t] for t in range(level.lanes // 128)]
        u[pl.ds(G, level.rows), :] += jnp.concatenate(tiles, axis=1)
        if depth:
            sweep(level, u, v, a)
            sweep(level, v, u, a)
        else:
            sweep(level, u, v, a)

            def put(r, rows, mid, new):
                out_ref[pl.ds(r - level.halo, rows.size), :] = new[:, :by]

            smooth(level, v, a, put, level.halo, bx)

    for exchange in (halo, halo_coef, halo_side):
        exchange.drain()
    for copy in sends:
        copy.wait_send()


def per_device(nx, ny, pressure, source, conductivity, storage):
    dx, dy = lax.axis_size("gx"), lax.axis_size("gy")
    bx, by = pressure.shape
    levels = [Level(depth, bx, by, nx, ny) for depth in range(LEVELS)]
    top, second, whole = levels[0], levels[1], levels[LOCAL]
    rows, tiles = bx >> LOCAL, by // 128
    scratch = [
        pltpu.VMEM((4, top.rows + 2 * G, top.lanes), F32),
        pltpu.VMEM((2, second.rows + 2 * G, second.lanes), F32),
        pltpu.VMEM((1, second.rows + 2 * G, second.lanes), F32),
        pltpu.VMEM((tiles, bx, 128), F32),
        pltpu.VMEM((2, tiles, bx, 128), F32),
        pltpu.VMEM((dy, rows * (by >> LOCAL) // 128, 128), F32),
        pltpu.VMEM((whole.rows, whole.lanes), F32),
        pltpu.VMEM((dy, rows, 128), F32),
        pltpu.VMEM((2, whole.rows, whole.lanes), F32),
    ]
    for level, count in ((top, 4), (second, 2), (second, 1)):
        scratch += Exchange.scratch(level, count)
    for level in levels:
        scratch += level.scratch()
    pairs = list(zip(levels, levels[1:]))
    scratch += [
        pltpu.VMEM((fine.lanes, coarse.lanes) if fine.depth else (by, by // 2), jnp.bfloat16)
        for fine, coarse in pairs
    ]
    scratch += [pltpu.VMEM((coarse.lanes, fine.lanes), jnp.bfloat16) for fine, coarse in pairs]
    scratch += [
        pltpu.SemaphoreType.DMA((4 + 2 * tiles,)),
        pltpu.SemaphoreType.DMA((2 * dy,)),
        pltpu.SemaphoreType.DMA((2 * dy,)),
        pltpu.SemaphoreType.DMA((3 * dx,)),
        pltpu.SemaphoreType.DMA((3 * dx,)),
    ]
    result = pl.pallas_call(
        functools.partial(kernel, levels, dx, dy),
        out_shape=jax.ShapeDtypeStruct((bx, by), F32),
        in_specs=[pl.BlockSpec(memory_space=pltpu.HBM)] * 4,
        out_specs=pl.BlockSpec(memory_space=pltpu.VMEM),
        scratch_shapes=scratch,
        compiler_params=pltpu.CompilerParams(
            collective_id=0, has_side_effects=True, vmem_limit_bytes=428 * 2**17
        ),
    )(pressure, source, conductivity, storage)
    return result


def solution(mesh):
    placed = (P("gx", "gy"), P("gx", "gy"), P("gx", "gy"), P("gx", "gy"))

    def run(pressure, source, conductivity, storage):
        nx, ny = pressure.shape
        return jax.shard_map(
            functools.partial(per_device, nx, ny),
            mesh=mesh, in_specs=placed, out_specs=P("gx", "gy"), check_vma=False,
        )(pressure, source, conductivity, storage)

    return run
```

```python
import functools

import jax
import jax.numpy as jnp
from jax import lax
from jax.experimental import pallas as pl
from jax.experimental.pallas import tpu as pltpu
from jax.sharding import PartitionSpec as P

LEVELS_SPLIT = 4
LEVELS_MERGED = 2
COARSE_SWEEPS = 8
OMEGA = 0.8

LOCAL = LEVELS_SPLIT - 1
LEVELS = LEVELS_SPLIT + LEVELS_MERGED
HALOS = (8, 16, 8)
G = 8
MESH = pl.DeviceIdType.MESH
F32 = jnp.float32


def round_up(n, m):
    return -(-n // m) * m


def iota(shape, dim):
    return lax.broadcasted_iota(jnp.int32, shape, dim)


def ones_where(mask):
    return jnp.where(mask, 1.0, 0.0).astype(jnp.bfloat16)


def parts(x):
    high = x.astype(jnp.bfloat16)
    low = (x - high.astype(F32)).astype(jnp.bfloat16)
    return high, low


def dot(a, b):
    return jnp.dot(a, b, preferred_element_type=F32)


def left(matrix, x):
    high, low = parts(x)
    return dot(matrix, high) + dot(matrix, low)


def right(x, matrix):
    high, low = parts(x)
    return dot(high, matrix) + dot(low, matrix)


def put_tiles(ref, rows, x):
    for t in range(x.shape[1] // 128):
        ref[t, rows, :] = x[:, 128 * t : 128 * t + 128]


def pair_rows(ref):
    tiles, rows, _ = ref.shape
    first, second = pl.ds(0, rows // 2, stride=2), pl.ds(1, rows // 2, stride=2)
    return jnp.concatenate([ref[t, first, :] + ref[t, second, :] for t in range(tiles)], axis=1)


def repeat_rows(ref, x):
    tiles, rows, _ = ref.shape
    for t in range(tiles):
        part = x[:, 128 * t : 128 * t + 128]
        ref[t, pl.ds(0, rows // 2, stride=2), :] = part
        ref[t, pl.ds(1, rows // 2, stride=2), :] = part


class Level:
    def __init__(self, depth, bx, by, nx, ny):
        self.depth = depth
        self.split = depth < LOCAL
        self.nx, self.ny = nx >> depth, ny >> depth
        if self.split:
            self.halo = HALOS[depth]
            self.bx, self.by = bx >> depth, by >> depth
            self.rows = self.bx + 2 * self.halo
            self.lanes = round_up(self.by + 2 * self.halo, 128)
        else:
            self.halo = 0
            self.bx, self.by = self.nx, self.ny
            self.rows = self.nx
            self.lanes = round_up(self.ny, 128)
        self.step = 32 if self.lanes > 128 else 128

    def scratch(self):
        tall = pltpu.VMEM((self.rows + 2 * G, self.lanes), F32)
        flat = pltpu.VMEM((self.rows, self.lanes), F32)
        tiled = (self.lanes // 128, self.rows, 128)
        return [
            pltpu.VMEM((7, self.rows, self.lanes), F32), tall, tall, tall, flat,
            pltpu.VMEM(tiled, F32), pltpu.VMEM((2, *tiled), F32),
        ]


def neighbours(win, count, lanes):
    mid = win[G : G + count]
    size = count + 2 * G
    up = pltpu.roll(win, 1, 0)[G : G + count]
    down = pltpu.roll(win, size - 1, 0)[G : G + count]
    before = pltpu.roll(mid, 1, 1)
    after = pltpu.roll(mid, lanes - 1, 1)
    return mid, up, down, before, after


def loop(start, count, step, body):
    for r in range(0, count, step):
        body(start + r, min(step, count - r))


def setup(level, k_ref, s_ref, a_ref, pairs=None, source=None):
    def body(r, count):
        mid, up, down, before, after = neighbours(
            k_ref[pl.ds(r, count + 2 * G), :], count, level.lanes
        )
        inside = mid > 0.0
        if not level.split:
            lane = iota(mid.shape, 1)
            before = jnp.where(lane == 0, 0.0, before)
            after = jnp.where(lane == level.lanes - 1, 0.0, after)
        west, east = 0.5 * (mid + up), 0.5 * (mid + down)
        south, north = 0.5 * (mid + before), 0.5 * (mid + after)
        rows = pl.ds(r, count)
        stored = s_ref[rows, :]
        diag = stored + west + east + south + north
        c = jnp.where(inside, OMEGA / diag, 0.0)
        a_ref[0, rows, :] = c * west
        a_ref[1, rows, :] = c * east
        if level.split:
            a_ref[2, rows, :] = c * south
            a_ref[3, rows, :] = c * north
        else:
            a_ref[2, rows, :] = jnp.where(lane == 0, 0.0, c * south)
            a_ref[3, rows, :] = jnp.where(lane == level.ny - 1, 0.0, c * north)
        a_ref[5, rows, :] = c
        a_ref[6, rows, :] = diag * (1.0 / OMEGA)
        if pairs is not None:
            put_tiles(pairs.at[0], rows, mid)
            put_tiles(pairs.at[1], rows, stored)
        if source is not None:
            a_ref[4, rows, :] = c * source[rows_of(r, count), :]

    loop(0, level.rows, level.step, body)


def rows_of(r, count):
    return pl.ds(r + G, count)


def smooth(level, src, a_ref, put, start=0, total=None):
    def body(r, count):
        mid, up, down, before, after = neighbours(
            src[pl.ds(r, count + 2 * G), :], count, level.lanes
        )
        rows = pl.ds(r, count)
        new = (1.0 - OMEGA) * mid + a_ref[4, rows, :]
        new = new + (a_ref[0, rows, :] * up + a_ref[1, rows, :] * down)
        new = new + (a_ref[2, rows, :] * before + a_ref[3, rows, :] * after)
        put(r, rows, mid, new)

    loop(start, level.rows if total is None else total, level.step, body)


def sweep(level, src, dst, a_ref, start=0, total=None):
    def put(r, rows, mid, new):
        dst[rows_of(r, rows.size), :] = new

    smooth(level, src, a_ref, put, start, total)


def residual(level, src, dst, a_ref):
    def put(r, rows, mid, new):
        put_tiles(dst, rows, (new - mid) * a_ref[6, rows, :])

    smooth(level, src, a_ref, put)


def residual_own(level, src, dst, a_ref):
    def put(r, rows, mid, new):
        part = (new - mid) * a_ref[6, rows, :]
        put_tiles(dst, pl.ds(r - level.halo, rows.size), part[:, : level.by])

    smooth(level, src, a_ref, put, level.halo, level.bx)


def lane_map(fine, coarse, lane):
    half = lane // 2
    if fine.split:
        shift = coarse.lanes - fine.lanes // 2
        half = jnp.where(lane >= fine.lanes - fine.halo, half + shift, half)
    return half


def matrices(fine, coarse, my):
    shape = (fine.by, coarse.by) if fine.depth == 0 else (fine.lanes, coarse.lanes)
    lane, there = iota(shape, 0), iota(shape, 1)
    if fine.depth == 0:
        down = lane // 2 == there
    elif fine.split and not coarse.split:
        down = (lane < fine.by) & (lane // 2 == there)
    else:
        down = lane_map(fine, coarse, lane) == there
    shape = (coarse.lanes, fine.lanes)
    there, lane = iota(shape, 0), iota(shape, 1)
    if fine.split and not coarse.split:
        col = jnp.where(lane >= fine.lanes - fine.halo, lane - fine.lanes, lane)
        gap = (lane >= fine.by + fine.halo) & (lane < fine.lanes - fine.halo)
        target = (col + my * fine.by + 2 * coarse.lanes) // 2 - coarse.lanes
        up = (there == target) & ~gap
    else:
        up = there == lane_map(fine, coarse, lane)
    return ones_where(down), ones_where(up)


def block_sum(x, count, factor, place):
    shape = (count, x.shape[0])
    rows = ones_where(iota(shape, 1) // factor == iota(shape, 0))
    shape = (x.shape[1], 128)
    cols = ones_where(iota(shape, 0) // factor + place == iota(shape, 1))
    return right(left(rows, x), cols)


class Exchange:
    def __init__(self, ext, scratch, level, here, size):
        self.ext, self.level = ext, level
        self.strips, self.halos = scratch[:2], scratch[2:4]
        self.mx, self.my = here
        self.dx, self.dy = size
        self.count, self.width = ext.shape[0], level.halo
        self.groups = 128 // (self.count * self.width)
        self.rows = level.bx // self.groups
        self.copies = []
        bx, by, w, rows = level.bx, level.by, self.width, self.rows
        for n, (sx, sy) in enumerate((i, j) for i in (-1, 0, 1) for j in (-1, 0, 1) if i or j):
            if sy == 0:
                first = G + w if sx < 0 else G + bx
                there = G + w + bx if sx < 0 else G
                src = ext.at[:, pl.ds(first, w), pl.ds(0, by)]
                dst = ext.at[:, pl.ds(there, w), pl.ds(0, by)]
            else:
                mine, theirs = (self.strips[0], self.halos[1]) if sy < 0 else (self.strips[1], self.halos[0])
                if sx == 0:
                    src, dst = mine, theirs.at[pl.ds(w, rows)]
                elif sx < 0:
                    src, dst = mine.at[pl.ds(0, w)], theirs.at[pl.ds(w + rows, w)]
                else:
                    src, dst = mine.at[pl.ds(rows - w, w)], theirs.at[pl.ds(0, w)]
            copy = pltpu.make_async_remote_copy(
                src_ref=src, dst_ref=dst, send_sem=scratch[4].at[n], recv_sem=scratch[5].at[n],
                device_id=(self.mx + sx, self.my + sy), device_id_type=MESH,
            )
            self.copies.append((copy, self.there(sx, sy), self.there(-sx, -sy)))

    @staticmethod
    def scratch(level, count):
        rows = level.bx * level.halo * count // 128
        strip, halo = pltpu.VMEM((rows, 128), F32), pltpu.VMEM((rows + 2 * level.halo, 128), F32)
        return [strip, strip, halo, halo, pltpu.SemaphoreType.DMA((8,)), pltpu.SemaphoreType.DMA((8,))]

    def there(self, sx, sy):
        x, y = self.mx + sx, self.my + sy
        return (x >= 0) & (x < self.dx) & (y >= 0) & (y < self.dy)

    def pack(self):
        level, w = self.level, self.width
        slot = iota((self.rows, 128), 1) // w
        for strip, first, at in ((self.strips[0], 0, 0), (self.strips[1], level.by - 128, 128 - w)):
            packed = None
            for i in range(self.count * self.groups):
                group, j = divmod(i, self.count)
                x = self.ext[j, pl.ds(G + w + group * self.rows, self.rows), pl.ds(first, 128)]
                turn = (w * i - at) % 128
                if turn:
                    x = pltpu.roll(x, turn, 1)
                packed = x if packed is None else jnp.where(slot == i, x, packed)
            strip[...] = packed

    def start(self):
        for copy, ok, _ in self.copies:
            pl.when(ok)(copy.start)

    def finish(self):
        for copy, _, back in self.copies:
            pl.when(back)(copy.wait_recv)
        level, w, rows = self.level, self.width, self.rows
        tile = pl.ds(level.lanes - 128, 128)
        blocks = [(0, w, self.groups - 1, G), (w + rows, w, 0, G + w + level.bx)]
        blocks += [(w, rows, g, G + w + g * rows) for g in range(self.groups)]
        for first, count, group, there in blocks:
            lower, upper = (ref[pl.ds(first, count), :] for ref in self.halos)
            lane = iota((count, 128), 1)
            right_part = (lane < w) & (self.my < self.dy - 1)
            left_part = (lane >= 128 - w) & (self.my > 0)
            for j in range(self.count):
                at = (group * self.count + j) * w
                turn_l, turn_r = (128 - w - at) % 128, -at % 128
                x = pltpu.roll(lower, turn_l, 1) if turn_l else lower
                y = pltpu.roll(upper, turn_r, 1) if turn_r else upper
                x = jnp.where(right_part, y, jnp.where(left_part, x, 0.0))
                self.ext[j, pl.ds(there, count), tile] = x
        for edge, first in ((self.mx == 0, G), (self.mx == self.dx - 1, G + w + level.bx)):
            @pl.when(edge)
            def _():
                self.ext[:, pl.ds(first, w), :] = jnp.zeros((self.count, w, level.lanes), F32)

    def drain(self):
        for copy, ok, _ in self.copies:
            pl.when(ok)(copy.wait_send)


def kernel(levels, dx, dy, *refs):
    p_hbm, s_hbm, k_hbm, st_hbm, out_ref = refs[:5]
    ext, ext_coef, ext_side, own_res, own_pairs, ga, gb, gca, gcb = refs[5:14]
    refs = refs[14:]
    ex_scratch, refs = [refs[:6], refs[6:12], refs[12:18]], refs[18:]
    held = []
    for _ in levels:
        held.append(list(refs[:7]))
        refs = refs[7:]
    downs, ups = refs[: LEVELS - 1], refs[LEVELS - 1 : 2 * LEVELS - 2]
    refs = refs[2 * LEVELS - 2 :]
    load_sem, y_send, y_recv, x_send, x_recv = refs

    mx, my = lax.axis_index("gx"), lax.axis_index("gy")
    top, second = levels[:2]
    bx, by = top.bx, top.by
    own = pl.ds(G + top.halo, bx)
    held[1][3], held[1][4] = ext_coef.at[0], ext_coef.at[1, pl.ds(G, second.rows)]

    loads, tiled_loads = [], []
    for i, ref in enumerate((p_hbm, s_hbm, k_hbm, st_hbm)):
        loads.append(pltpu.make_async_copy(ref, ext.at[i, own, pl.ds(0, by)], load_sem.at[i]))
        loads[-1].start()
    for i, ref in enumerate((k_hbm, st_hbm)):
        for t in range(by // 128):
            tiled_loads.append(pltpu.make_async_copy(
                ref.at[:, pl.ds(128 * t, 128)], own_pairs.at[i, t], load_sem.at[4 + i * (by // 128) + t]
            ))
            tiled_loads[-1].start()

    halo = Exchange(ext, ex_scratch[0], top, (mx, my), (dx, dy))
    halo_coef = Exchange(ext_coef, ex_scratch[1], second, (mx, my), (dx, dy))
    halo_side = Exchange(ext_side, ex_scratch[2], second, (mx, my), (dx, dy))

    barrier = pltpu.get_barrier_semaphore()
    for d in range(1, dx):
        pl.semaphore_signal(barrier, inc=1, device_id=(lax.rem(mx + d, dx), my), device_id_type=MESH)
    for d in range(1, dy):
        pl.semaphore_signal(barrier, inc=1, device_id=(mx, lax.rem(my + d, dy)), device_id_type=MESH)
    signals = dx - 1 + dy - 1
    for sx in (-1, 1):
        for sy in (-1, 1):
            ok = halo.there(sx, sy)
            signals = signals + jnp.where(ok, 1, 0)
            @pl.when(ok)
            def _():
                pl.semaphore_signal(barrier, inc=1, device_id=(mx + sx, my + sy), device_id_type=MESH)

    for ref, level in ((ext.at[0], top), (ext.at[2], top), (ext_coef.at[0], second)):
        ref[0:G, :] = jnp.zeros((G, level.lanes), F32)
        ref[G + level.rows :, :] = jnp.zeros((G, level.lanes), F32)
    for level, (a, v, u, k, s, r, c) in zip(levels, held):
        for ref in (v, u, k):
            ref[0:G, :] = jnp.zeros((G, level.lanes), F32)
            ref[G + level.rows :, :] = jnp.zeros((G, level.lanes), F32)
    downs[0][...] = matrices(top, second, my)[0]

    for copy in loads:
        copy.wait()
    halo.pack()
    pl.semaphore_wait(barrier, signals)
    halo.start()

    for copy in tiled_loads:
        copy.wait()
    half = bx // 2
    own_second = pl.ds(G + second.halo, half)
    both = jnp.concatenate([pair_rows(own_pairs.at[0]), pair_rows(own_pairs.at[1])], axis=0)
    both = right(both, downs[0][...])
    near_k, near_s = 0.5 * both[:half], both[half:]
    ext_coef[0, own_second, 0 : by // 2] = near_k
    ext_coef[1, own_second, 0 : by // 2] = near_s

    whole = levels[LOCAL]
    factor = 1 << LOCAL
    gx_rows, gy_cols = bx // factor, by // factor
    sends = []

    def send(src, dst, sems, n, target):
        copy = pltpu.make_async_remote_copy(
            src_ref=src, dst_ref=dst, send_sem=sems[0].at[n], recv_sem=sems[1].at[n],
            device_id=target, device_id_type=MESH,
        )
        copy.start()
        sends.append(copy)
        return copy

    def over_gy(buffer, base):
        return [
            send(buffer.at[my], buffer.at[my], (y_send, y_recv), base + d, (mx, lax.rem(my + d, dy)))
            for d in range(1, dy)
        ]

    def strip_of(row):
        return pl.ds(pl.multiple_of(row * gx_rows, 8), gx_rows)

    far_k = 0.5 ** (LOCAL - 1) * block_sum(near_k, gx_rows, factor // 2, 0)
    gca[my] = far_k + block_sum(near_s, gx_rows, factor // 2, gy_cols)
    coef_y = over_gy(gca, 0)
    halo_coef.pack()
    halo_coef.start()

    for depth in range(1, LOCAL):
        downs[depth][...] = matrices(levels[depth], levels[depth + 1], my)[0]

    halo.finish()
    setup(top, ext.at[2], ext.at[3, pl.ds(G, top.rows)], held[0][0], None, ext.at[1])

    for copy in coef_y:
        copy.wait_recv()

    def merge(ref, i):
        shape = (ref.shape[1], whole.lanes)
        lane = iota(shape, 1)
        merged = jnp.zeros(shape, F32)
        for j in range(dy):
            first = gy_cols * j
            x = jnp.concatenate([ref[j]] * (whole.lanes // 128), axis=1)
            turn = (first - gy_cols * i) % whole.lanes
            x = pltpu.roll(x, turn, 1) if turn else x
            merged = jnp.where((lane >= first) & (lane < first + gy_cols), x, merged)
        return merged

    for i in range(2):
        gcb[i, strip_of(mx), :] = merge(gca, i)
    mine = gcb.at[:, strip_of(mx)]
    coef_x = [
        send(mine, mine, (x_send, x_recv), d, (lax.rem(mx + d, dx), my)) for d in range(2, dx, 2)
    ]

    def coarse_terms(depth):
        level = levels[depth]
        a, _, _, k, s, _, pairs = held[depth]
        fine = held[depth - 1][6]
        both = jnp.concatenate([pair_rows(fine.at[0]), pair_rows(fine.at[1])], axis=0)
        both = right(both, downs[depth - 1][...])
        k[pl.ds(G, level.rows), :] = 0.5 * both[: level.rows]
        s[...] = both[level.rows :]
        needed = depth != LOCAL - 1 and depth != LEVELS - 1
        setup(level, k, s, a, pairs if needed else None)

    def first_sweep(depth, side):
        level = levels[depth]
        a, v = held[depth][:2]
        first = a[5] * side
        a[4] = first
        v[pl.ds(G, level.rows), :] = first

    sweep(top, ext.at[0], held[0][1], held[0][0])
    sweep(top, held[0][1], held[0][2], held[0][0])
    residual_own(top, held[0][2], own_res, held[0][0])
    ext_side[0, own_second, 0 : by // 2] = right(pair_rows(own_res), downs[0][...])
    halo_side.pack()
    halo_side.start()

    halo_coef.finish()
    setup(second, held[1][3], held[1][4], held[1][0], held[1][6])
    for depth in range(2, LOCAL):
        coarse_terms(depth)
    for copy in coef_x:
        copy.wait_recv()
    core = lax.rem(mx, 2)
    coef_x = []
    for chip in range(dx // 2):
        part = gcb.at[:, strip_of(2 * chip + core)]
        coef_x.append(send(part, part, (x_send, x_recv), 2 * dx + chip, (mx + 1 - 2 * core, my)))

    halo_side.finish()
    for depth in range(1, LOCAL):
        level = levels[depth]
        a, v, u, k, s, res, _ = held[depth]
        if depth == 1:
            first_sweep(depth, ext_side[0, pl.ds(G, level.rows), :])
        else:
            first_sweep(depth, right(pair_rows(held[depth - 1][5]), downs[depth - 1][...]))
        sweep(level, v, u, a)
        residual(level, u, res, a)

    last = levels[LOCAL - 1]
    edge = last.halo // 2
    side = right(pair_rows(held[LOCAL - 1][5]), downs[LOCAL - 1][...])
    packed = 128 // gy_cols
    count = gx_rows // packed
    strip = side[edge : edge + count, :128]
    for g in range(1, packed):
        strip = strip + pltpu.roll(side[edge + g * count : edge + (g + 1) * count, :128], g * gy_cols, 1)
    ga[my] = strip
    side_y = over_gy(ga, dy)

    for copy in coef_x:
        copy.wait_recv()
    a, _, _, k, s, _, pairs = held[LOCAL]
    k[pl.ds(G, whole.rows), :] = gcb[0]
    s[...] = gcb[1]
    setup(whole, k, s, a, pairs)

    for copy in side_y:
        copy.wait_recv()
    for g in range(packed):
        gb[pl.ds(pl.multiple_of(mx * gx_rows + g * count, 8), count), :] = merge(ga, g)
    mine = gb.at[strip_of(mx)]
    side_x = [
        send(mine, mine, (x_send, x_recv), dx + d, (lax.rem(mx + d, dx), my)) for d in range(2, dx, 2)
    ]
    mate = (mx + 1 - 2 * core, my)
    relayed = [send(mine, mine, (x_send, x_recv), 3 * dx, mate)]

    for depth in range(LEVELS - 1):
        down, ups[depth][...] = matrices(levels[depth], levels[depth + 1], my)
        if depth >= LOCAL:
            downs[depth][...] = down
    for depth in range(LOCAL + 1, LEVELS):
        coarse_terms(depth)

    for d, copy in zip(range(2, dx, 2), side_x):
        copy.wait_recv()
        part = gb.at[strip_of(lax.rem(mx - d + dx, dx))]
        relayed.append(send(part, part, (x_send, x_recv), 3 * dx + d, mate))
    for copy in relayed:
        copy.wait_recv()

    for depth in range(LOCAL, LEVELS):
        level = levels[depth]
        a, v, u, k, s, res, _ = held[depth]
        if depth == LOCAL:
            first_sweep(depth, gb[...])
        else:
            first_sweep(depth, right(pair_rows(held[depth - 1][5]), downs[depth - 1][...]))
        if depth < LEVELS - 1:
            sweep(level, v, u, a)
            residual(level, u, res, a)
        else:
            for i in range(COARSE_SWEEPS - 1):
                sweep(level, *((v, u) if i % 2 == 0 else (u, v)), a)
            if COARSE_SWEEPS % 2:
                u[...] = v[...]

    for depth in reversed(range(LEVELS - 1)):
        level, below = levels[depth], levels[depth + 1]
        a, v, u, k, s, res, _ = held[depth]
        error = held[depth + 1][2]
        if depth == LOCAL - 1:
            window = error[pl.ds(pl.multiple_of(mx * gx_rows, 8), gx_rows + 2 * G), :]
            wide = right(window, ups[depth][...])[G - edge : G + gx_rows + edge]
        else:
            skip = below.halo - level.halo // 2
            wide = right(error[pl.ds(G + skip, below.rows - 2 * skip), :], ups[depth][...])
        repeat_rows(res, wide)
        tiles = [res[t] for t in range(level.lanes // 128)]
        u[pl.ds(G, level.rows), :] += jnp.concatenate(tiles, axis=1)
        if depth:
            sweep(level, u, v, a)
            sweep(level, v, u, a)
        else:
            sweep(level, u, v, a)

            def put(r, rows, mid, new):
                out_ref[pl.ds(r - level.halo, rows.size), :] = new[:, :by]

            smooth(level, v, a, put, level.halo, bx)

    for exchange in (halo, halo_coef, halo_side):
        exchange.drain()
    for copy in sends:
        copy.wait_send()


def per_device(nx, ny, pressure, source, conductivity, storage):
    dx, dy = lax.axis_size("gx"), lax.axis_size("gy")
    bx, by = pressure.shape
    levels = [Level(depth, bx, by, nx, ny) for depth in range(LEVELS)]
    top, second, whole = levels[0], levels[1], levels[LOCAL]
    rows, tiles = bx >> LOCAL, by // 128
    scratch = [
        pltpu.VMEM((4, top.rows + 2 * G, top.lanes), F32),
        pltpu.VMEM((2, second.rows + 2 * G, second.lanes), F32),
        pltpu.VMEM((1, second.rows + 2 * G, second.lanes), F32),
        pltpu.VMEM((tiles, bx, 128), F32),
        pltpu.VMEM((2, tiles, bx, 128), F32),
        pltpu.VMEM((dy, rows * (by >> LOCAL) // 128, 128), F32),
        pltpu.VMEM((whole.rows, whole.lanes), F32),
        pltpu.VMEM((dy, rows, 128), F32),
        pltpu.VMEM((2, whole.rows, whole.lanes), F32),
    ]
    for level, count in ((top, 4), (second, 2), (second, 1)):
        scratch += Exchange.scratch(level, count)
    for level in levels:
        scratch += level.scratch()
    pairs = list(zip(levels, levels[1:]))
    scratch += [
        pltpu.VMEM((fine.lanes, coarse.lanes) if fine.depth else (by, by // 2), jnp.bfloat16)
        for fine, coarse in pairs
    ]
    scratch += [pltpu.VMEM((coarse.lanes, fine.lanes), jnp.bfloat16) for fine, coarse in pairs]
    scratch += [
        pltpu.SemaphoreType.DMA((4 + 2 * tiles,)),
        pltpu.SemaphoreType.DMA((2 * dy,)),
        pltpu.SemaphoreType.DMA((2 * dy,)),
        pltpu.SemaphoreType.DMA((4 * dx,)),
        pltpu.SemaphoreType.DMA((4 * dx,)),
    ]
    result = pl.pallas_call(
        functools.partial(kernel, levels, dx, dy),
        out_shape=jax.ShapeDtypeStruct((bx, by), F32),
        in_specs=[pl.BlockSpec(memory_space=pltpu.HBM)] * 4,
        out_specs=pl.BlockSpec(memory_space=pltpu.VMEM),
        scratch_shapes=scratch,
        compiler_params=pltpu.CompilerParams(
            collective_id=0, has_side_effects=True, vmem_limit_bytes=428 * 2**17
        ),
    )(pressure, source, conductivity, storage)
    return result


def solution(mesh):
    placed = (P("gx", "gy"), P("gx", "gy"), P("gx", "gy"), P("gx", "gy"))

    def run(pressure, source, conductivity, storage):
        nx, ny = pressure.shape
        return jax.shard_map(
            functools.partial(per_device, nx, ny),
            mesh=mesh, in_specs=placed, out_specs=P("gx", "gy"), check_vma=False,
        )(pressure, source, conductivity, storage)

    return run
```
